256 devices in a mesh: dp: 8 (over y, core), ctx: 16 (over z, x_hi), tp: 2 (over x_lo).
Axes of the slice: x: 4 (x_hi: 2, x_lo: 2; x = x_hi * 2 + x_lo), y: 4, z: 8, core: 2. Of those that a mesh axis runs over, the one named last changes fastest.
Arguments:
- queries: bfloat16 [32, 1024, 2048], P('dp', 'ctx', 'tp'), may hold values from -8 to 8
- key_states: bfloat16 [32, 1024, 1024], P('dp', 'ctx', 'tp'), may hold values from -8 to 8
- value_state_rows: bfloat16 [32, 1024, 1024], P('dp', 'ctx', 'tp'), may hold values from -6 to 6
- segment_ids: int32 [32, 1024], P('dp', 'ctx'), may hold values from 0 to 3, never falling along the last dimension, each value on 1 to 512 neighbouring positions
- output_grad: bfloat16 [32, 1024, 3584], P('dp', 'ctx', 'tp'), may hold values from -6 to 6
- out_weight: bfloat16 [2048, 3584], P('tp'), may hold values from -0.09375 to 0.09375
- destination: int32 [32], replicated, may hold values from 0 to 31, as said below
Outputs:
- query_out: bfloat16 [32, 1024, 2048], P('dp', 'ctx', 'tp')
- key_out: bfloat16 [32, 1024, 1024], P('dp', 'ctx', 'tp')
- value_out: bfloat16 [32, 1024, 1024], P('dp', 'ctx', 'tp')
The draws below stay inside these ranges and needn't reach their ends.
Inputs may be any that keep to these rules, and one draw needn't show every extreme that they name: `segment_ids`: ids never fall along a row; each document holds 1 to 512 positions, some document exactly 512. `destination`: a permutation of the rows; rows r // 4 == g form data group g, and the 4 rows of one group go to 4 different groups.
All inputs are finite; a program needn't handle non-finite values.
Results may differ from the reference program's by a relative error of at most 0.015.
Values may be sent and summed in bfloat16 or wider, within the bound.
No kernel may reach another device: no remote copies, remote signals or barrier semaphores. Data moves between devices by JAX's collectives and lax.ppermute only.
A program may use at most 128 MiB of HBM per device.

```python
import math
import jax
import jax.numpy as jnp
import numpy as np
from jax import lax

D = 3584
HEAD_SIZE = 256
QUERY_HEADS = 8
KEY_VALUE_HEADS = 4
ROWS = 4
BLOCK = 64
PACKED_LENGTH = 1024
TOTAL_SEQUENCES = 32
N_CTX = 16


def shared_direction(key):
    return jax.random.rademacher(jax.random.fold_in(key, 101), (KEY_VALUE_HEADS, HEAD_SIZE), dtype=jnp.float32)


def drawn_field(key, array_shape, lowest, highest):
    mask_key, amp_key = jax.random.split(key)
    chosen = (jax.random.randint(mask_key, array_shape, 0, 8) == 0).astype(jnp.float32)
    amplitude = jax.random.uniform(amp_key, array_shape, jnp.float32, lowest, highest)
    return chosen * amplitude


def draw_queries(key, part):
    direction = shared_direction(key)
    key = jax.random.fold_in(key, 3)
    noise_key, field_key = jax.random.split(key)
    query_group_size = QUERY_HEADS // KEY_VALUE_HEADS
    array_shape = (TOTAL_SEQUENCES, PACKED_LENGTH, KEY_VALUE_HEADS, query_group_size)
    noise = jax.random.truncated_normal(noise_key, -6.0, 6.0, array_shape + (HEAD_SIZE,), jnp.float32)
    field = drawn_field(field_key, array_shape, 1.2, 1.8)
    value_entries = noise + field[..., None] * direction[None, None, :, None, :]
    return value_entries.reshape(TOTAL_SEQUENCES, PACKED_LENGTH, QUERY_HEADS * HEAD_SIZE).astype(jnp.bfloat16)


def draw_key_states(key, part):
    direction = shared_direction(key)
    key = jax.random.fold_in(key, 5)
    noise_key, field_key = jax.random.split(key)
    array_shape = (TOTAL_SEQUENCES, PACKED_LENGTH, KEY_VALUE_HEADS)
    noise = jax.random.truncated_normal(noise_key, -6.0, 6.0, array_shape + (HEAD_SIZE,), jnp.float32)
    field = drawn_field(field_key, array_shape, 1.2, 1.8)
    value_entries = noise + field[..., None] * direction[None, None, :, :]
    return value_entries.reshape(TOTAL_SEQUENCES, PACKED_LENGTH, KEY_VALUE_HEADS * HEAD_SIZE).astype(jnp.bfloat16)


def draw_destination(key, part):
    key = jax.random.fold_in(key, 7)
    first_key, second_key, third_key = jax.random.split(key, 3)
    group_count = TOTAL_SEQUENCES // ROWS
    ordering = jax.random.permutation(first_key, group_count).astype(jnp.int32)
    shuffled = (jax.random.permutation(second_key, group_count - 1) + 1).astype(jnp.int32)
    offsets = jnp.concatenate([jnp.zeros((1,), jnp.int32), shuffled[:ROWS - 1]])
    source_group = jnp.arange(group_count, dtype=jnp.int32)[:, None]
    target = ordering[(source_group + offsets[None, :]) % group_count]
    row_scores = jax.random.randint(third_key, (group_count, ROWS), 0, 1 << 20) * ROWS + jnp.arange(ROWS, dtype=jnp.int32)[None, :]
    slot_order = jnp.argsort(row_scores, axis=1).astype(jnp.int32)
    slots = slot_order[target, jnp.arange(ROWS, dtype=jnp.int32)[None, :]]
    return (target * ROWS + slots).reshape(TOTAL_SEQUENCES).astype(jnp.int32)


def block_scale(own_key, dims, cuts, low, high):
    def one(dim, shards_of):
        steps = jax.random.uniform(jax.random.fold_in(jax.random.fold_in(own_key, 6), dim), (shards_of,), jnp.float32, low / len(cuts), high / len(cuts))
        return jnp.repeat(jnp.exp(steps), dims[dim] // shards_of).reshape((-1,) + (1,) * (len(dims) - dim - 1))

    loudness = one(*cuts[0])
    for cut in cuts[1:]:
        loudness = loudness * one(*cut)
    return loudness


def split_up(amount, total, limit, slope):
    portions = [(1 << 20) // math.isqrt(grade ** slope) + 1 for grade in range(2, amount + 1)]
    surplus, given = total - limit - (amount - 1), [1] * (amount - 1)
    while surplus > 0:
        movable = [i for i in range(amount - 1) if given[i] < limit]
        whole, remaining = sum([portions[i] for i in movable]), surplus
        for i in movable:
            addition = min(limit - given[i], max(1, remaining * portions[i] // whole), surplus)
            given[i] = given[i] + addition
            surplus = surplus - addition
    return np.array([limit] + given)


def uneven_parts(own_key, amount, total, most, lean):
    if amount == 2:
        one = jax.random.randint(own_key, (), max(1, total - most), min(most, total - 1) + 1)
        return jnp.stack([one, total - one])
    sizes = jnp.asarray(split_up(amount, total, most, lean), jnp.int32)
    twos = (amount - 1) // 2
    source_of, receiver = sizes[1:1 + 2 * twos:2], sizes[2:2 + 2 * twos:2]
    margin = jnp.minimum(source_of - 1, most - receiver)
    passed = jax.random.randint(jax.random.fold_in(own_key, 1), (twos,), 0, 1 << 20) % (margin + 1)
    sizes = sizes.at[1:1 + 2 * twos:2].set(source_of - passed).at[2:2 + 2 * twos:2].set(receiver + passed)
    return sizes[jax.random.permutation(jax.random.fold_in(own_key, 2), amount)]


def normal_values(stream_key, dims, spread, limit, shards=(), held_as=jnp.bfloat16):
    factor_of = block_scale(stream_key, dims, shards, -0.22, 0.18) if shards else 1.0
    values = jax.random.normal(stream_key, dims, jnp.float32) * spread * factor_of
    return jnp.minimum(jnp.maximum(values, -limit), limit).astype(held_as)


def setup_inputs(seed: int = 0) -> dict:
    splits = jax.random.split(jax.random.key(seed), 8)
    queries = draw_queries(jax.random.fold_in(splits[7], 71), 0)
    key_states = draw_key_states(jax.random.fold_in(splits[7], 71), 0)
    value_state_rows = normal_values(splits[2], (TOTAL_SEQUENCES, PACKED_LENGTH, KEY_VALUE_HEADS * HEAD_SIZE), 1.0, 6.0, ((0, 8), (1, 16), (2, 2)))
    segment_ids = jax.vmap(lambda own: jnp.searchsorted(jnp.cumsum(uneven_parts(own, 4, PACKED_LENGTH, PACKED_LENGTH // 2, 2)), jnp.arange(PACKED_LENGTH), side="right"))(jax.random.split(splits[3], TOTAL_SEQUENCES)).reshape((TOTAL_SEQUENCES, PACKED_LENGTH)).astype(jnp.int32)
    output_grad = normal_values(splits[4], (TOTAL_SEQUENCES, PACKED_LENGTH, D), 1.0, 6.0, ((0, 8), (1, 16), (2, 2)))
    out_weight = normal_values(splits[5], (QUERY_HEADS * HEAD_SIZE, D), D ** -0.5, 0.09375, ((0, 2),))
    destination = draw_destination(jax.random.fold_in(splits[7], 71), 0)
    return dict(queries=queries, key_states=key_states, value_state_rows=value_state_rows, segment_ids=segment_ids, output_grad=output_grad, out_weight=out_weight, destination=destination)


logit_cap = 50.0
score_scale = 0.0625


def narrowed(values_f32):
    return lax.optimization_barrier(values_f32.astype(jnp.bfloat16)).astype(jnp.float32)


def reference(queries, key_states, value_state_rows, segment_ids, output_grad, out_weight, destination):
    query_group_size = QUERY_HEADS // KEY_VALUE_HEADS
    weight_f32 = out_weight.astype(jnp.float32)
    key_index = jnp.arange(PACKED_LENGTH, dtype=jnp.int32)

    def one_row(operands):
        single_query_row, single_key_row, single_value_row, segment_row, grad_row = operands
        attention_gradient = jnp.einsum('td,hd->th', grad_row.astype(jnp.float32), weight_f32).astype(jnp.bfloat16)
        query_head_rows = single_query_row.astype(jnp.float32).reshape(PACKED_LENGTH, KEY_VALUE_HEADS, query_group_size, HEAD_SIZE)
        head_gradients = attention_gradient.astype(jnp.float32).reshape(PACKED_LENGTH, KEY_VALUE_HEADS, query_group_size, HEAD_SIZE)
        key_head_rows = single_key_row.astype(jnp.float32).reshape(PACKED_LENGTH, KEY_VALUE_HEADS, HEAD_SIZE)
        value_head_rows = single_value_row.astype(jnp.float32).reshape(PACKED_LENGTH, KEY_VALUE_HEADS, HEAD_SIZE)

        def query_block(accumulated, block_index):
            key_acc, value_acc = accumulated
            first_row = (block_index * BLOCK).astype(jnp.int32)
            block_query = lax.dynamic_slice_in_dim(query_head_rows, first_row, BLOCK, 0)
            block_grad = lax.dynamic_slice_in_dim(head_gradients, first_row, BLOCK, 0)
            block_segment = lax.dynamic_slice_in_dim(segment_row, first_row, BLOCK, 0)
            positions = first_row + jnp.arange(BLOCK, dtype=jnp.int32)
            allowed = (block_segment[:, None] == segment_row[None, :]) & (key_index[None, :] <= positions[:, None])
            raw_scores = jnp.einsum('ckgd,lkd->kgcl', block_query, key_head_rows) * score_scale
            capped = logit_cap * jnp.tanh(raw_scores / logit_cap)
            exponent_terms = jnp.where(allowed, jnp.exp(capped), 0.0)
            exp_total = jnp.sum(exponent_terms, axis=-1)
            unnorm = jnp.einsum('kgcl,lkd->ckgd', narrowed(exponent_terms), value_head_rows)
            attn_out = unnorm / jnp.transpose(exp_total, (2, 0, 1))[..., None]
            row_delta = jnp.sum(block_grad * attn_out, axis=-1)
            attn_prob = jnp.where(allowed, jnp.exp(capped - jnp.log(exp_total)[..., None]), 0.0)
            prob_grad = jnp.einsum('ckgd,lkd->kgcl', block_grad, value_head_rows)
            score_grad = attn_prob * (prob_grad - jnp.transpose(row_delta, (1, 2, 0))[..., None])
            raw_grad = narrowed(score_grad * (1.0 - (capped / logit_cap) ** 2) * score_scale)
            prob_low = narrowed(attn_prob)
            query_grad = jnp.einsum('kgcl,lkd->ckgd', raw_grad, key_head_rows).astype(jnp.bfloat16)
            key_part = narrowed(jnp.einsum('kgcl,ckgd->lkd', raw_grad, block_query))
            value_part = narrowed(jnp.einsum('kgcl,ckgd->lkd', prob_low, block_grad))
            return (key_acc + key_part, value_acc + value_part), query_grad

        initial_sums = (jnp.zeros((PACKED_LENGTH, KEY_VALUE_HEADS, HEAD_SIZE), jnp.float32), jnp.zeros((PACKED_LENGTH, KEY_VALUE_HEADS, HEAD_SIZE), jnp.float32))
        partial_sums, query_blocks = lax.scan(query_block, initial_sums, jnp.arange(N_CTX, dtype=jnp.int32))
        query_grads = query_blocks.reshape(PACKED_LENGTH, QUERY_HEADS * HEAD_SIZE)
        key_gradient_rows = partial_sums[0].astype(jnp.bfloat16).reshape(PACKED_LENGTH, KEY_VALUE_HEADS * HEAD_SIZE)
        value_gradient_rows = partial_sums[1].astype(jnp.bfloat16).reshape(PACKED_LENGTH, KEY_VALUE_HEADS * HEAD_SIZE)
        return query_grads, key_gradient_rows, value_gradient_rows

    query_all, key_all, value_all = lax.map(one_row, (queries, key_states, value_state_rows, segment_ids, output_grad))
    query_out = jnp.zeros_like(query_all).at[destination].set(query_all)
    key_out = jnp.zeros_like(key_all).at[destination].set(key_all)
    value_out = jnp.zeros_like(value_all).at[destination].set(value_all)
    return query_out, key_out, value_out
```

```python
import functools

import jax
import jax.numpy as jnp
from jax import lax
from jax.experimental import pallas as pl
from jax.experimental.pallas import tpu as pltpu
from jax.sharding import PartitionSpec as P

HEAD = 256
CAP = 50.0
SCALE = 0.0625
LOG2E = 1.4426950408889634
F32 = jnp.float32
BF16 = jnp.bfloat16
VMEM_LIMIT = 48 * 1024 * 1024


def dot(a, b, ca, cb):
    return lax.dot_general(a, b, (((ca,), (cb,)), ((), ())), preferred_element_type=F32)


def projection_kernel(tp_ref, own_ref, other_ref, weight_ref, out_ref):
    rows, block, half = own_ref.shape
    tp = tp_ref[0]
    own_at = pl.multiple_of(tp * half, 128)
    other_at = pl.multiple_of((1 - tp) * half, 128)
    own = own_ref[...].reshape(rows * block, half)
    other = other_ref[...].reshape(rows * block, half)
    total = dot(own, weight_ref[:, pl.ds(own_at, half)], 1, 1)
    total += dot(other, weight_ref[:, pl.ds(other_at, half)], 1, 1)
    out_ref[...] = total.astype(BF16).reshape(out_ref.shape)


def project(own, other, weight, tp):
    rows, block, half = own.shape
    heads = weight.shape[0] // HEAD
    whole = pl.BlockSpec((rows, block, half), lambda h, tp: (0, 0, 0))
    return pl.pallas_call(
        projection_kernel,
        grid_spec=pltpu.PrefetchScalarGridSpec(
            num_scalar_prefetch=1,
            grid=(heads,),
            in_specs=[
                whole,
                whole,
                pl.BlockSpec((HEAD, 2 * half), lambda h, tp: (h, 0)),
            ],
            out_specs=pl.BlockSpec(
                (rows, 1, block, HEAD), lambda h, tp: (0, h // 2, 0, h % 2)
            ),
        ),
        out_shape=jax.ShapeDtypeStruct((rows, heads // 2, block, 2 * HEAD), BF16),
        compiler_params=pltpu.CompilerParams(vmem_limit_bytes=VMEM_LIMIT),
        cost_estimate=pl.CostEstimate(
            flops=2 * rows * block * 2 * half * heads * HEAD,
            bytes_accessed=2 * heads * HEAD * 2 * half,
            transcendentals=0,
        ),
        name="project",
    )(tp, own, other, weight)


def attention_kernel(
    q_ref, kv_own, kv_other, do_ref, qinfo, kinfo, dq_ref, dkv_own, dkv_other, acc
):
    steps, block, _ = q_ref.shape
    per = 2
    lanes = per * block
    acc[...] = jnp.zeros_like(acc)

    def heads_on_rows(ref, z):
        both = ref[z : z + per].reshape(lanes, 2 * HEAD)
        return jnp.concatenate([both[:, :HEAD], both[:, HEAD:]], axis=0)

    for z in range(0, steps, per):
        low, high = max(0, z - 4), z + per
        q = heads_on_rows(q_ref, z)
        do = heads_on_rows(do_ref, z)
        seg_q = qinfo[0:1, z * block : z * block + lanes]
        pos_q = qinfo[1:2, z * block : z * block + lanes]
        parts = []
        total = 0.0
        weighted = 0.0
        for side, kv_ref in ((0, kv_own), (1, kv_other)):
            kv = kv_ref[low:high].reshape((high - low) * block, 2 * HEAD)
            k, v = kv[:, :HEAD], kv[:, HEAD:]
            seg_k = kinfo[side, low * block : high * block, 0:1]
            pos_k = kinfo[side, low * block : high * block, 1:2]
            allowed = (seg_k == seg_q) & (pos_k <= pos_q)
            allowed = jnp.concatenate([allowed, allowed], axis=1)
            t = jnp.tanh(dot(k, q, 1, 1) * (SCALE / CAP))
            e = jnp.where(allowed, jnp.exp2(t * (CAP * LOG2E)), 0.0)
            dp = dot(v, do, 1, 1)
            total += jnp.sum(e, axis=0, keepdims=True)
            weighted += jnp.sum(e.astype(BF16).astype(F32) * dp, axis=0, keepdims=True)
            parts.append((k, t, e, dp))
        inverse = 1.0 / total
        delta = weighted * inverse
        scaled = inverse * SCALE
        dq = 0.0
        for side, (k, t, e, dp) in enumerate(parts):
            prob = (e * inverse).astype(BF16)
            ds = ((e * scaled) * (dp - delta) * (1.0 - t * t)).astype(BF16)
            acc[side, low * block : high * block, :HEAD] += dot(ds, q, 1, 0)
            acc[side, low * block : high * block, HEAD:] += dot(prob, do, 1, 0)
            dq += dot(ds, k, 0, 0)
        dq = dq.astype(BF16)
        dq_ref[z : z + per, :, :HEAD] = dq[:lanes].reshape(per, block, HEAD)
        dq_ref[z : z + per, :, HEAD:] = dq[lanes:].reshape(per, block, HEAD)
    dkv_own[...] = acc[0].reshape(dkv_own.shape)
    dkv_other[...] = acc[1].astype(BF16).reshape(dkv_other.shape)


def attention(q, kv_own, kv_other, do, qinfo, kinfo):
    steps, block, width = q.shape
    vmem = pl.BlockSpec(memory_space=pltpu.VMEM)
    return pl.pallas_call(
        attention_kernel,
        in_specs=[vmem] * 6,
        out_specs=[vmem] * 3,
        out_shape=[
            jax.ShapeDtypeStruct((steps, block, width), BF16),
            jax.ShapeDtypeStruct((steps, block, width), F32),
            jax.ShapeDtypeStruct((steps, block, width), BF16),
        ],
        scratch_shapes=[pltpu.VMEM((2, steps * block, width), F32)],
        compiler_params=pltpu.CompilerParams(vmem_limit_bytes=VMEM_LIMIT),
        cost_estimate=pl.CostEstimate(
            flops=3 * 10**9, bytes_accessed=6 * 2**20, transcendentals=1200000
        ),
        name="attend",
    )(q, kv_own, kv_other, do, qinfo, kinfo)


def copy_kernel(index_ref, in_ref, out_ref):
    out_ref[...] = in_ref[...]


def pick_rows(index, source):
    count, rest = index.shape[0], source.shape[1:]
    zeros = (0,) * len(rest)
    return pl.pallas_call(
        copy_kernel,
        grid_spec=pltpu.PrefetchScalarGridSpec(
            num_scalar_prefetch=1,
            grid=(count,),
            in_specs=[pl.BlockSpec((1,) + rest, lambda i, index: (index[i],) + zeros)],
            out_specs=pl.BlockSpec((1,) + rest, lambda i, index: (i,) + zeros),
        ),
        out_shape=jax.ShapeDtypeStruct((count,) + rest, source.dtype),
        name="pick",
    )(index, source)


def place_q_kernel(index_ref, in_ref, out_ref):
    width = in_ref.shape[-1]
    for h in range(in_ref.shape[1]):
        out_ref[0, :, h * width : (h + 1) * width] = in_ref[0, h]


def place_kv_kernel(index_ref, in_ref, key_ref, value_ref):
    for h in range(in_ref.shape[1]):
        key_ref[0, :, h * HEAD : (h + 1) * HEAD] = in_ref[0, h, :, :HEAD]
        value_ref[0, :, h * HEAD : (h + 1) * HEAD] = in_ref[0, h, :, HEAD:]


def place_rows(kernel, index, source, out_widths, name):
    count = index.shape[0]
    rest = source.shape[1:]
    block = source.shape[2]
    return pl.pallas_call(
        kernel,
        grid_spec=pltpu.PrefetchScalarGridSpec(
            num_scalar_prefetch=1,
            grid=(count,),
            in_specs=[pl.BlockSpec((1,) + rest, lambda i, index: (index[i], 0, 0, 0))],
            out_specs=[
                pl.BlockSpec((1, block, w), lambda i, index: (i, 0, 0))
                for w in out_widths
            ],
        ),
        out_shape=[
            jax.ShapeDtypeStruct((count, block, w), source.dtype) for w in out_widths
        ],
        name=name,
    )(index, source)


def exchange(x, axis, groups=None):
    return lax.all_to_all(
        x, axis, split_axis=0, concat_axis=0, tiled=True, axis_index_groups=groups
    )


def on_device(
    queries, key_states, value_state_rows, segment_ids, output_grad, out_weight, destination
):
    rows, block, q_width = queries.shape
    kv_heads = key_states.shape[2] // HEAD
    units = rows * kv_heads
    n_ctx = lax.axis_size("ctx")
    groups = lax.axis_size("dp")
    pair = n_ctx // units
    ctx = lax.axis_index("ctx")
    tp = lax.axis_index("tp")
    group = lax.axis_index("dp")
    side = ctx % pair
    unit = ctx // pair
    columns = [[z * pair + h for z in range(units)] for h in range(pair)]
    swap = [(z * pair + h, z * pair + 1 - h) for z in range(units) for h in range(pair)]

    dest = destination.reshape(groups, rows)
    own_targets = lax.dynamic_slice_in_dim(dest, group, 1, 0) // rows
    send_index = jnp.sum(
        jnp.where(
            own_targets == jnp.arange(groups, dtype=jnp.int32)[:, None],
            jnp.arange(rows, dtype=jnp.int32)[None, :],
            0,
        ),
        axis=1,
    )
    wanted = group * rows + jnp.arange(rows, dtype=jnp.int32)
    recv_index = jnp.sum(
        jnp.where(
            destination[None, :] == wanted[:, None],
            jnp.arange(groups * rows, dtype=jnp.int32)[None, :] // rows,
            0,
        ),
        axis=1,
    )

    other_grad = lax.ppermute(output_grad, "tp", [(0, 1), (1, 0)])

    def per_unit(x):
        x = x.reshape(rows, block, kv_heads, x.shape[2] // kv_heads)
        return jnp.transpose(x, (0, 2, 1, 3)).reshape(units, block, x.shape[3])

    kv = jnp.concatenate([per_unit(key_states), per_unit(value_state_rows)], axis=2)
    kv_own = exchange(kv, "ctx", columns)
    q = exchange(per_unit(queries), "ctx", columns)
    kv_other = lax.ppermute(kv_own, "ctx", swap)

    seg_send = jnp.repeat(segment_ids, kv_heads * pair, axis=0)
    seg_all = exchange(seg_send, "ctx").reshape(units, pair, block)
    pos_all = jnp.arange(n_ctx * block, dtype=jnp.int32).reshape(units, pair, block)

    def of_side(x, which):
        return lax.dynamic_slice_in_dim(x, which, 1, 1).reshape(units * block)

    info = [
        jnp.stack([of_side(seg_all, which), of_side(pos_all, which)])
        for which in (side, 1 - side)
    ]
    qinfo = info[0]
    kinfo = jnp.stack([jnp.transpose(info[0]), jnp.transpose(info[1])])

    do = project(output_grad, other_grad, out_weight, tp[None].astype(jnp.int32))
    do = exchange(do.reshape(units, block, q_width // kv_heads), "ctx", columns)

    dq, dkv_mine, dkv_theirs = attention(q, kv_own, kv_other, do, qinfo, kinfo)

    dq = exchange(dq, "ctx", columns)
    dkv_back = lax.ppermute(dkv_theirs, "ctx", swap)
    dkv = (dkv_mine + dkv_back.astype(F32)).astype(BF16)
    dkv = exchange(dkv, "ctx", columns)

    def by_row(x):
        return x.reshape(rows, kv_heads, block, x.shape[2])

    dq = exchange(pick_rows(send_index, by_row(dq)), "dp")
    (query_out,) = place_rows(place_q_kernel, recv_index, dq, [q_width], "place_q")
    dkv = exchange(pick_rows(send_index, by_row(dkv)), "dp")
    key_out, value_out = place_rows(
        place_kv_kernel, recv_index, dkv, [kv_heads * HEAD] * 2, "place_kv"
    )
    return query_out, key_out, value_out


def solution(mesh):
    in_specs = (
        P("dp", "ctx", "tp"),
        P("dp", "ctx", "tp"),
        P("dp", "ctx", "tp"),
        P("dp", "ctx"),
        P("dp", "ctx", "tp"),
        P("tp", None),
        P(),
    )
    out_specs = (P("dp", "ctx", "tp"), P("dp", "ctx", "tp"), P("dp", "ctx", "tp"))
    return jax.shard_map(
        on_device, mesh=mesh, in_specs=in_specs, out_specs=out_specs, check_vma=False
    )
```

```python
import jax
import jax.numpy as jnp
from jax import lax
from jax.experimental import pallas as pl
from jax.experimental.pallas import tpu as pltpu
from jax.sharding import PartitionSpec as P

HEAD = 256
CAP = 50.0
SCALE = 0.0625
LOG2E = 1.4426950408889634
F32 = jnp.float32
BF16 = jnp.bfloat16
TILE = 16
SMALL_VMEM = 8 * 1024 * 1024
WHOLE_VMEM = 60 * 1024 * 1024
LARGE_VMEM = 28 * 1024 * 1024


def dot(a, b, ca, cb):
    return lax.dot_general(a, b, (((ca,), (cb,)), ((), ())), preferred_element_type=F32)


VMEM = pl.BlockSpec(memory_space=pltpu.VMEM)
SMEM = pl.BlockSpec(memory_space=pltpu.SMEM)
ANY = pl.BlockSpec(memory_space=pl.ANY)


def pack_kernel(seg_ref, q_hbm, k_hbm, v_hbm, out_ref, q_ref, k_ref, v_ref, sems):
    rows, block, q_width = q_ref.shape
    kv_heads = k_ref.shape[2] // HEAD
    width = q_width // kv_heads
    pieces = block // TILE
    copies = [
        pltpu.make_async_copy(source, target, sems.at[i])
        for i, (source, target) in enumerate(
            ((q_hbm, q_ref), (k_hbm, k_ref), (v_hbm, v_ref))
        )
    ]
    for copy in copies:
        copy.start()
    place = lax.broadcasted_iota(jnp.int32, (TILE, block), 1)
    row = lax.broadcasted_iota(jnp.int32, (TILE, block), 0)
    lane = lax.broadcasted_iota(jnp.int32, (TILE, 128), 1)
    ids = []
    for r in range(rows):
        spread = jnp.broadcast_to(seg_ref[r : r + 1], (TILE, block)).astype(F32)
        columns = jnp.zeros((TILE, 128), F32)
        for j in range(pieces):
            column = jnp.sum(
                jnp.where(place == row + j * TILE, spread, 0.0), axis=1, keepdims=True
            )
            columns = jnp.where(lane == j, column, columns)
        ids.append(columns.astype(BF16))
    for copy in copies:
        copy.wait()
    for r in range(rows):
        for h in range(kv_heads):
            u = r * kv_heads + h
            heads = slice(h * HEAD, (h + 1) * HEAD)
            for j in range(pieces):
                at = slice(j * TILE, (j + 1) * TILE)
                k_at = pieces * HEAD + j * 2 * HEAD
                out_ref[u, :, j * HEAD : (j + 1) * HEAD] = q_ref[
                    r, at, h * width : h * width + HEAD
                ]
                out_ref[u, :, k_at : k_at + HEAD] = k_ref[r, at, heads]
                out_ref[u, :, k_at + HEAD : k_at + 2 * HEAD] = v_ref[r, at, heads]
            out_ref[u, :, pieces * 3 * HEAD :] = ids[r]


def pack(seg, q, k, v):
    rows, block, _ = q.shape
    kv_heads = k.shape[2] // HEAD
    lanes = block // TILE * 3 * HEAD + 128
    return pl.pallas_call(
        pack_kernel,
        in_specs=[VMEM, ANY, ANY, ANY],
        out_specs=VMEM,
        out_shape=jax.ShapeDtypeStruct((rows * kv_heads, TILE, lanes), BF16),
        scratch_shapes=[
            pltpu.VMEM(q.shape, BF16),
            pltpu.VMEM(k.shape, BF16),
            pltpu.VMEM(v.shape, BF16),
            pltpu.SemaphoreType.DMA((3,)),
        ],
        compiler_params=pltpu.CompilerParams(vmem_limit_bytes=WHOLE_VMEM),
        name="pack",
    )(seg, q, k, v)


def own_half_kernel(index_ref, x_ref, weight_ref, out_ref, turned_ref):
    rows, block, half = x_ref.shape
    x = x_ref[...].reshape(rows * block, half)
    own = pl.multiple_of(index_ref[0] * half, 128)
    other = pl.multiple_of((1 - index_ref[0]) * half, 128)
    for h in range(weight_ref.shape[0] // HEAD):
        at = slice(h * HEAD, (h + 1) * HEAD)
        out_ref[:, at] = dot(x, weight_ref[at, pl.ds(own, half)], 1, 1)
        turned_ref[:, at] = weight_ref[at, pl.ds(other, half)].T


def project_own(x, weight, index):
    rows, block, half = x.shape
    width = weight.shape[0]
    return pl.pallas_call(
        own_half_kernel,
        in_specs=[SMEM, VMEM, VMEM],
        out_specs=[VMEM, VMEM],
        out_shape=[
            jax.ShapeDtypeStruct((rows * block, width), F32),
            jax.ShapeDtypeStruct((half, width), BF16),
        ],
        compiler_params=pltpu.CompilerParams(vmem_limit_bytes=LARGE_VMEM),
        cost_estimate=pl.CostEstimate(
            flops=2 * rows * block * half * width,
            bytes_accessed=4 * half * width,
            transcendentals=0,
        ),
        name="project_own",
    )(index, x, weight)


def other_half_kernel(x_ref, turned_ref, part_ref, q_ref, out_ref):
    rows, block, half = x_ref.shape
    kv_heads = out_ref.shape[1]
    width = turned_ref.shape[1] // kv_heads
    x = x_ref[...].reshape(rows * block, half)
    for h in range(kv_heads):
        at = slice(h * width, (h + 1) * width)
        total = part_ref[:, at] + dot(x, turned_ref[:, at], 1, 0)
        out_ref[:, h, :, :width] = total.astype(BF16).reshape(rows, block, width)
        out_ref[:, h, :, width:] = q_ref[:, :, h * width + HEAD : (h + 1) * width]


def project_other(x, turned, part, q, kv_heads):
    rows, block, half = x.shape
    width = turned.shape[1]
    return pl.pallas_call(
        other_half_kernel,
        in_specs=[VMEM] * 4,
        out_specs=VMEM,
        out_shape=jax.ShapeDtypeStruct(
            (rows, kv_heads, block, 2 * width // kv_heads - HEAD), BF16
        ),
        compiler_params=pltpu.CompilerParams(vmem_limit_bytes=LARGE_VMEM),
        cost_estimate=pl.CostEstimate(
            flops=2 * 10**10, bytes_accessed=2 * half * width, transcendentals=0
        ),
        name="project_other",
    )(x, turned, part, q)


def attention_kernel(
    side_ref, own_ref, other_ref, do_ref, dq_ref, dkv_own, dkv_other, acc
):
    steps, block, width = dq_ref.shape
    per = 2
    lanes = per * block
    pieces = block // TILE
    side = side_ref[0]
    acc[...] = jnp.zeros_like(acc)

    def gathered(ref, low, high, start, stride, size):
        return jnp.concatenate(
            [
                ref[z, :, start + j * stride : start + j * stride + size]
                for z in range(low, high)
                for j in range(pieces)
            ],
            axis=0,
        )

    def ids(ref, low, high, start):
        return jnp.concatenate(
            [
                ref[z, :, start : start + 128].astype(F32)[:, j : j + 1]
                for z in range(low, high)
                for j in range(pieces)
            ],
            axis=0,
        )

    def positions(shape, axis, low, which):
        n = lax.broadcasted_iota(jnp.int32, shape, axis)
        return 2 * n - (n & (block - 1)) + (per * block * low + block * which)

    q_end = pieces * HEAD
    diagonal = lax.broadcasted_iota(
        jnp.int32, (lanes, lanes), 0
    ) == lax.broadcasted_iota(jnp.int32, (lanes, lanes), 1)

    for z in range(0, steps, per):
        low, high = max(0, z - 4), z + per
        keys = (high - low) * block
        do = do_ref[z:high].reshape(lanes, width + HEAD)
        q = jnp.concatenate(
            [gathered(own_ref, z, high, 0, HEAD, HEAD), do[:, width:]], axis=0
        )
        do = jnp.concatenate([do[:, :HEAD], do[:, HEAD:width]], axis=0)
        seg_q = ids(own_ref, z, high, q_end + pieces * 2 * HEAD)
        seg_q = jnp.sum(jnp.where(diagonal, seg_q, 0.0), axis=0, keepdims=True)
        pos_q = positions((1, lanes), 1, z, side)
        parts = []
        total = 0.0
        weighted = 0.0
        for which, ref, start in ((0, own_ref, q_end), (1, other_ref, 0)):
            k = gathered(ref, low, high, start, 2 * HEAD, HEAD)
            v = gathered(ref, low, high, start + HEAD, 2 * HEAD, HEAD)
            seg_k = ids(ref, low, high, start + pieces * 2 * HEAD)
            key_side = side if which == 0 else 1 - side
            pos_k = positions((keys, lanes), 0, low, key_side)
            allowed = (seg_k == seg_q) & (pos_k <= pos_q)
            allowed = jnp.concatenate([allowed, allowed], axis=1)
            t = jnp.tanh(dot(k, q, 1, 1) * (SCALE / CAP))
            e = jnp.where(allowed, jnp.exp2(t * (CAP * LOG2E)), 0.0)
            dp = dot(v, do, 1, 1)
            total += jnp.sum(e, axis=0, keepdims=True)
            weighted += jnp.sum(e.astype(BF16).astype(F32) * dp, axis=0, keepdims=True)
            parts.append((k, t, e, dp))
        inverse = 1.0 / total
        delta = weighted * inverse
        scaled = inverse * SCALE
        dq = 0.0
        for which, (k, t, e, dp) in enumerate(parts):
            prob = (e * inverse).astype(BF16)
            ds = ((e * scaled) * (dp - delta) * (1.0 - t * t)).astype(BF16)
            acc[which, low * block : high * block, :HEAD] += dot(ds, q, 1, 0)
            acc[which, low * block : high * block, HEAD:] += dot(prob, do, 1, 0)
            dq += dot(ds, k, 0, 0)
        dq = dq.astype(BF16)
        dq_ref[z:high, :, :HEAD] = dq[:lanes].reshape(per, block, HEAD)
        dq_ref[z:high, :, HEAD:] = dq[lanes:].reshape(per, block, HEAD)
    dkv_own[...] = acc[0].reshape(dkv_own.shape)
    dkv_other[...] = acc[1].astype(BF16).reshape(dkv_other.shape)


def attention(side, own, other, do):
    steps, block, width = do.shape
    width -= HEAD
    return pl.pallas_call(
        attention_kernel,
        in_specs=[SMEM, VMEM, VMEM, VMEM],
        out_specs=[VMEM] * 3,
        out_shape=[
            jax.ShapeDtypeStruct((steps, block, width), BF16),
            jax.ShapeDtypeStruct((steps, block, width), F32),
            jax.ShapeDtypeStruct((steps, block, width), BF16),
        ],
        scratch_shapes=[pltpu.VMEM((2, steps * block, width), F32)],
        compiler_params=pltpu.CompilerParams(vmem_limit_bytes=LARGE_VMEM),
        cost_estimate=pl.CostEstimate(
            flops=3 * 10**9, bytes_accessed=6 * 2**20, transcendentals=1200000
        ),
        name="attend",
    )(side, own, other, do)


def run_copies(copies):
    for copy in copies:
        copy.start()
    for copy in copies:
        copy.wait()


def pick_kernel(index_ref, in_ref, *outs):
    for i, out in enumerate(outs):
        out[...] = in_ref[index_ref[i]]


def pick_rows(index, source):
    count, rest = index.shape[0], source.shape[1:]
    return pl.pallas_call(
        pick_kernel,
        in_specs=[SMEM, VMEM],
        out_specs=[VMEM] * count,
        out_shape=[jax.ShapeDtypeStruct(rest, source.dtype)] * count,
        compiler_params=pltpu.CompilerParams(vmem_limit_bytes=SMALL_VMEM),
        name="pick",
    )(index, source)


def pick_stacked_kernel(index_ref, in_ref, out_ref, sems):
    run_copies(
        [
            pltpu.make_async_copy(in_ref.at[index_ref[i]], out_ref.at[i], sems.at[i])
            for i in range(out_ref.shape[0])
        ]
    )


def pick_stacked(index, source):
    count, rest = index.shape[0], source.shape[1:]
    return pl.pallas_call(
        pick_stacked_kernel,
        in_specs=[SMEM, VMEM],
        out_specs=ANY,
        out_shape=jax.ShapeDtypeStruct((count,) + rest, source.dtype),
        scratch_shapes=[pltpu.SemaphoreType.DMA((count,))],
        compiler_params=pltpu.CompilerParams(vmem_limit_bytes=SMALL_VMEM),
        name="pick_stacked",
    )(index, source)


def place_q_kernel(index_ref, *refs):
    ins, out_ref, sems = refs[:-2], refs[-2], refs[-1]
    kv_heads, _, width = ins[0].shape

    def copy(source, s, h):
        return pltpu.make_async_copy(
            source.at[h], out_ref.at[s, :, pl.ds(h * width, width)], sems.at[s, h]
        )

    for s in range(out_ref.shape[0]):
        for i, source in enumerate(ins):

            @pl.when(index_ref[s] == i)
            def _():
                for h in range(kv_heads):
                    copy(source, s, h).start()

    for s in range(out_ref.shape[0]):
        for h in range(kv_heads):
            copy(ins[0], s, h).wait()


def place_q(index, sources):
    count = index.shape[0]
    kv_heads, block, width = sources[0].shape
    return pl.pallas_call(
        place_q_kernel,
        in_specs=[SMEM] + [VMEM] * len(sources),
        out_specs=ANY,
        out_shape=jax.ShapeDtypeStruct((count, block, kv_heads * width), BF16),
        scratch_shapes=[pltpu.SemaphoreType.DMA((count, kv_heads))],
        compiler_params=pltpu.CompilerParams(vmem_limit_bytes=SMALL_VMEM),
        name="place_q",
    )(index, *sources)


def place_kv_kernel(index_ref, in_ref, key_ref, value_ref, sems):
    copies = []
    for s in range(key_ref.shape[0]):
        for h in range(in_ref.shape[1]):
            for w, out_ref in enumerate((key_ref, value_ref)):
                copies.append(
                    pltpu.make_async_copy(
                        in_ref.at[index_ref[s], h, :, pl.ds(w * HEAD, HEAD)],
                        out_ref.at[s, :, pl.ds(h * HEAD, HEAD)],
                        sems.at[s, h, w],
                    )
                )
    run_copies(copies)


def place_kv(index, source):
    count = index.shape[0]
    _, kv_heads, block, _ = source.shape
    return pl.pallas_call(
        place_kv_kernel,
        in_specs=[SMEM, VMEM],
        out_specs=[ANY] * 2,
        out_shape=[jax.ShapeDtypeStruct((count, block, kv_heads * HEAD), BF16)] * 2,
        scratch_shapes=[pltpu.SemaphoreType.DMA((count, kv_heads, 2))],
        compiler_params=pltpu.CompilerParams(vmem_limit_bytes=SMALL_VMEM),
        name="place_kv",
    )(index, source)


def exchange(x, axis, groups=None):
    return lax.all_to_all(
        x, axis, split_axis=0, concat_axis=0, tiled=True, axis_index_groups=groups
    )


def on_device(
    queries, key_states, value_state_rows, segment_ids, output_grad, out_weight, destination
):
    rows, block, q_width = queries.shape
    kv_heads = key_states.shape[2] // HEAD
    units = rows * kv_heads
    n_ctx = lax.axis_size("ctx")
    groups = lax.axis_size("dp")
    pair = n_ctx // units
    ctx = lax.axis_index("ctx")
    tp = lax.axis_index("tp")
    group = lax.axis_index("dp")
    side = ctx % pair
    columns = [[z * pair + h for z in range(units)] for h in range(pair)]
    swap = [(z * pair + h, z * pair + 1 - h) for z in range(units) for h in range(pair)]

    other_grad = lax.ppermute(output_grad, "tp", [(0, 1), (1, 0)])

    own = pack(segment_ids, queries, key_states, value_state_rows)
    own = exchange(own, "ctx", columns)
    other = lax.ppermute(own[:, :, block // TILE * HEAD :], "ctx", swap)

    def partner(g, i, sign):
        chips = groups // 2
        return (g // 2 + sign * (i // 2) + chips) % chips * 2 + (g % 2 + i) % 2

    steps = jnp.arange(groups, dtype=jnp.int32)
    dest = destination.reshape(groups, rows)
    own_targets = lax.dynamic_slice_in_dim(dest, group, 1, 0) // rows

    def row_for(targets):
        return jnp.sum(
            jnp.where(
                own_targets == targets[:, None],
                jnp.arange(rows, dtype=jnp.int32)[None, :],
                0,
            ),
            axis=1,
        )

    wanted = group * rows + jnp.arange(rows, dtype=jnp.int32)
    recv_index = jnp.sum(
        jnp.where(
            destination[None, :] == wanted[:, None],
            jnp.arange(groups * rows, dtype=jnp.int32)[None, :] // rows,
            0,
        ),
        axis=1,
    )
    recv_step = jnp.sum(
        jnp.where(recv_index[:, None] == partner(group, steps, -1)[None, :], steps, 0),
        axis=1,
    )
    send_index = row_for(steps)
    send_step = row_for(partner(group, steps, 1))

    index = tp[None].astype(jnp.int32)
    part, turned = project_own(output_grad, out_weight, index)
    do = project_other(other_grad, turned, part, queries, kv_heads)
    do = exchange(do.reshape(units, block, do.shape[3]), "ctx", columns)

    dq, dkv_mine, dkv_theirs = attention(
        side[None].astype(jnp.int32), own, other, do
    )

    dq = exchange(dq, "ctx", columns)
    dkv_back = lax.ppermute(dkv_theirs, "ctx", swap)
    dkv = (dkv_mine + dkv_back.astype(F32)).astype(BF16)
    dkv, dq = lax.optimization_barrier((dkv, dq))
    dkv = exchange(dkv, "ctx", columns)

    def by_row(x):
        return x.reshape(rows, kv_heads, block, x.shape[2])

    sent = pick_rows(send_step, by_row(dq))
    got = [sent[0]]
    for i in range(1, groups):
        route = [(g, partner(g, i, 1)) for g in range(groups)]
        got.append(lax.ppermute(sent[i], "dp", route))
    dkv, *got = lax.optimization_barrier((dkv, *got))
    query_out = place_q(recv_step, got)
    dkv = exchange(pick_stacked(send_index, by_row(dkv)), "dp")
    key_out, value_out = place_kv(recv_index, dkv)
    return query_out, key_out, value_out


def solution(mesh):
    in_specs = (
        P("dp", "ctx", "tp"),
        P("dp", "ctx", "tp"),
        P("dp", "ctx", "tp"),
        P("dp", "ctx"),
        P("dp", "ctx", "tp"),
        P("tp", None),
        P(),
    )
    out_specs = (P("dp", "ctx", "tp"), P("dp", "ctx", "tp"), P("dp", "ctx", "tp"))
    return jax.shard_map(
        on_device, mesh=mesh, in_specs=in_specs, out_specs=out_specs, check_vma=False
    )
```

```python
import jax
import jax.numpy as jnp
from jax import lax
from jax.experimental import pallas as pl
from jax.experimental.pallas import tpu as pltpu
from jax.sharding import PartitionSpec as P

HEAD = 256
CAP = 50.0
SCALE = 0.0625
LOG2E = 1.4426950408889634
F32 = jnp.float32
BF16 = jnp.bfloat16
TILE = 16
ORDER = (0, 2, 4, 6, 1, 3, 5, 7)
SLOT = tuple(ORDER.index(z) for z in range(len(ORDER)))
SMALL_VMEM = 8 * 1024 * 1024
LARGE_VMEM = 28 * 1024 * 1024


def dot(a, b, ca, cb):
    return lax.dot_general(a, b, (((ca,), (cb,)), ((), ())), preferred_element_type=F32)


VMEM = pl.BlockSpec(memory_space=pltpu.VMEM)
SMEM = pl.BlockSpec(memory_space=pltpu.SMEM)
ANY = pl.BlockSpec(memory_space=pl.ANY)


def pack_kernel(seg_hbm, k_hbm, v_hbm, out_ref, seg_ref, k_ref, v_ref, sems):
    rows, block, kv_width = k_ref.shape
    kv_heads = kv_width // HEAD
    pieces = block // TILE
    copies = [
        pltpu.make_async_copy(source, target, sems.at[i])
        for i, (source, target) in enumerate(
            ((seg_hbm, seg_ref), (k_hbm, k_ref), (v_hbm, v_ref))
        )
    ]
    for copy in copies:
        copy.start()
    copies[0].wait()
    place = lax.broadcasted_iota(jnp.int32, (TILE, block), 1)
    row = lax.broadcasted_iota(jnp.int32, (TILE, block), 0)
    lane = lax.broadcasted_iota(jnp.int32, (TILE, 128), 1)
    for r in range(rows):
        spread = jnp.broadcast_to(seg_ref[r : r + 1], (TILE, block)).astype(F32)
        columns = jnp.zeros((TILE, 128), F32)
        for j in range(pieces):
            column = jnp.sum(
                jnp.where(place == row + j * TILE, spread, 0.0), axis=1, keepdims=True
            )
            columns = jnp.where(lane == j, column, columns)
        for h in range(kv_heads):
            out_ref[r * kv_heads + h, :, pieces * 2 * HEAD :] = columns.astype(BF16)
    copies[1].wait()
    copies[2].wait()
    for r in range(rows):
        for h in range(kv_heads):
            u = r * kv_heads + h
            heads = slice(h * HEAD, (h + 1) * HEAD)
            for j in range(pieces):
                at = slice(j * TILE, (j + 1) * TILE)
                k_at = j * 2 * HEAD
                out_ref[u, :, k_at : k_at + HEAD] = k_ref[r, at, heads]
                out_ref[u, :, k_at + HEAD : k_at + 2 * HEAD] = v_ref[r, at, heads]


def pack(seg, k, v):
    rows, block, kv_width = k.shape
    kv_heads = kv_width // HEAD
    lanes = block // TILE * 2 * HEAD + 128
    return pl.pallas_call(
        pack_kernel,
        in_specs=[ANY] * 3,
        out_specs=VMEM,
        out_shape=jax.ShapeDtypeStruct((rows * kv_heads, TILE, lanes), BF16),
        scratch_shapes=[
            pltpu.VMEM(seg.shape, jnp.int32),
            pltpu.VMEM(k.shape, BF16),
            pltpu.VMEM(v.shape, BF16),
            pltpu.SemaphoreType.DMA((3,)),
        ],
        compiler_params=pltpu.CompilerParams(vmem_limit_bytes=SMALL_VMEM),
        name="pack",
    )(*(pltpu.with_memory_space_constraint(x, pltpu.HBM) for x in (seg, k, v)))


def own_half_kernel(index_ref, x_ref, weight_ref, out_ref, turned_ref):
    rows, block, half = x_ref.shape
    x = x_ref[...].reshape(rows * block, half)
    own = pl.multiple_of(index_ref[0] * half, 128)
    other = pl.multiple_of((1 - index_ref[0]) * half, 128)
    for h in range(weight_ref.shape[0] // HEAD):
        at = slice(h * HEAD, (h + 1) * HEAD)
        out_ref[:, at] = dot(x, weight_ref[at, pl.ds(own, half)], 1, 1)
        turned_ref[:, at] = weight_ref[at, pl.ds(other, half)].T


def project_own(x, weight, index):
    rows, block, half = x.shape
    width = weight.shape[0]
    return pl.pallas_call(
        own_half_kernel,
        in_specs=[SMEM, VMEM, VMEM],
        out_specs=[VMEM, VMEM],
        out_shape=[
            jax.ShapeDtypeStruct((rows * block, width), F32),
            jax.ShapeDtypeStruct((half, width), BF16),
        ],
        compiler_params=pltpu.CompilerParams(vmem_limit_bytes=LARGE_VMEM),
        cost_estimate=pl.CostEstimate(
            flops=2 * rows * block * half * width,
            bytes_accessed=4 * half * width,
            transcendentals=0,
        ),
        name="project_own",
    )(index, x, weight)


def other_half_kernel(x_ref, turned_ref, part_ref, q_ref, out_ref):
    rows, block, half = x_ref.shape
    kv_heads = out_ref.shape[1]
    width = turned_ref.shape[1] // kv_heads
    x = x_ref[...].reshape(rows * block, half)
    for h in range(kv_heads):
        at = slice(h * width, (h + 1) * width)
        out_ref[:, h, :, :width] = q_ref[:, :, at]
        total = part_ref[:, at] + dot(x, turned_ref[:, at], 1, 0)
        out_ref[:, h, :, width:] = total.astype(BF16).reshape(rows, block, width)


def project_other(x, turned, part, q, kv_heads):
    rows, block, half = x.shape
    total = turned.shape[1]
    return pl.pallas_call(
        other_half_kernel,
        in_specs=[VMEM] * 4,
        out_specs=VMEM,
        out_shape=jax.ShapeDtypeStruct(
            (rows, kv_heads, block, 2 * total // kv_heads), BF16
        ),
        compiler_params=pltpu.CompilerParams(vmem_limit_bytes=LARGE_VMEM),
        cost_estimate=pl.CostEstimate(
            flops=2 * rows * block * half * total,
            bytes_accessed=2 * half * total,
            transcendentals=0,
        ),
        name="project_other",
    )(x, turned, part, q)


def attention_kernel(
    side_ref, own_ref, other_ref, qd_ref, dq_ref, dkv_own, dkv_other, acc
):
    steps, block, width = dq_ref.shape
    per = 2
    lanes = per * block
    pieces = block // TILE
    side = side_ref[0]

    def gathered(ref, low, high, start):
        return jnp.concatenate(
            [
                ref[SLOT[z], :, start + j * 2 * HEAD : start + j * 2 * HEAD + HEAD]
                for z in range(low, high)
                for j in range(pieces)
            ],
            axis=0,
        )

    def ids(ref, low, high):
        return jnp.concatenate(
            [
                ref[SLOT[z], :, pieces * 2 * HEAD :].astype(F32)[:, j : j + 1]
                for z in range(low, high)
                for j in range(pieces)
            ],
            axis=0,
        )

    def positions(shape, axis, low, which):
        n = lax.broadcasted_iota(jnp.int32, shape, axis)
        return 2 * n - (n & (block - 1)) + (per * block * low + block * which)

    diagonal = lax.broadcasted_iota(
        jnp.int32, (lanes, lanes), 0
    ) == lax.broadcasted_iota(jnp.int32, (lanes, lanes), 1)

    for z in range(0, steps, per):
        low, high = max(0, z - 4), z + per
        qd = jnp.concatenate([qd_ref[SLOT[i]] for i in range(z, high)], axis=0)
        q = jnp.concatenate([qd[:, :HEAD], qd[:, HEAD:width]], axis=0)
        do = jnp.concatenate(
            [qd[:, width : width + HEAD], qd[:, width + HEAD :]], axis=0
        )
        seg_q = ids(own_ref, z, high)
        seg_q = jnp.sum(jnp.where(diagonal, seg_q, 0.0), axis=0, keepdims=True)
        pos_q = positions((1, lanes), 1, z, side)
        parts = []
        total = 0.0
        weighted = 0.0
        for which, ref in enumerate((own_ref, other_ref)):
            for start, stop in ((low, z), (z, high)):
                if start == stop:
                    continue
                k = gathered(ref, start, stop, 0)
                v = gathered(ref, start, stop, HEAD)
                allowed = ids(ref, start, stop) == seg_q
                if start == z:
                    key_side = side if which == 0 else 1 - side
                    pos_k = positions((lanes, lanes), 0, z, key_side)
                    allowed &= pos_k <= pos_q
                allowed = jnp.concatenate([allowed, allowed], axis=1)
                t = jnp.tanh(dot(k, q, 1, 1) * (SCALE / CAP))
                e = jnp.where(allowed, jnp.exp2(t * (CAP * LOG2E)), 0.0)
                dp = dot(v, do, 1, 1)
                total += jnp.sum(e, axis=0, keepdims=True)
                weighted += jnp.sum(e * dp, axis=0, keepdims=True)
                parts.append((which, start, stop, k, t, e, dp))
        inverse = 1.0 / total
        delta = weighted * inverse
        dq = 0.0
        for which, start, stop, k, t, e, dp in parts:
            prob = e * inverse
            ds = (prob * (dp - delta) * (1.0 - t * t)).astype(BF16)
            at = slice(start * block, stop * block)
            dk, dv = dot(ds, q, 1, 0), dot(prob.astype(BF16), do, 1, 0)
            if z == start:
                acc[which, at, :HEAD] = dk
                acc[which, at, HEAD:] = dv
            else:
                acc[which, at, :HEAD] += dk
                acc[which, at, HEAD:] += dv
            dq += dot(ds, k, 0, 0)
        dq *= SCALE
        dq = dq.astype(BF16)
        for i in range(per):
            at = slice(i * block, (i + 1) * block)
            dq_ref[SLOT[z + i], :, :HEAD] = dq[:lanes][at]
            dq_ref[SLOT[z + i], :, HEAD:] = dq[lanes:][at]
    for z in range(steps):
        at = slice(z * block, (z + 1) * block)
        for which, out_ref in enumerate((dkv_own, dkv_other)):
            out_ref[SLOT[z], :, :HEAD] = (acc[which, at, :HEAD] * SCALE).astype(BF16)
            out_ref[SLOT[z], :, HEAD:] = acc[which, at, HEAD:].astype(BF16)


def attention(side, own, other, q_and_grad):
    steps, block, width = q_and_grad.shape
    width //= 2
    return pl.pallas_call(
        attention_kernel,
        in_specs=[SMEM] + [VMEM] * 3,
        out_specs=[VMEM] * 3,
        out_shape=[
            pltpu.HBM((steps, block, width), BF16),
            pltpu.VMEM((steps, block, width), BF16),
            pltpu.VMEM((steps, block, width), BF16),
        ],
        scratch_shapes=[pltpu.VMEM((2, steps * block, width), F32)],
        compiler_params=pltpu.CompilerParams(vmem_limit_bytes=LARGE_VMEM),
        cost_estimate=pl.CostEstimate(
            flops=3 * 10**9, bytes_accessed=6 * 2**20, transcendentals=1200000
        ),
        name="attend",
    )(side, own, other, q_and_grad)


def run_copies(copies):
    for copy in copies:
        copy.start()
    for copy in copies:
        copy.wait()


def pick_kernel(index_ref, in_ref, *outs):
    for i, out in enumerate(outs):
        out[...] = in_ref[index_ref[i]]


def pick_rows(index, source):
    count, rest = index.shape[0], source.shape[1:]
    return pl.pallas_call(
        pick_kernel,
        in_specs=[SMEM, VMEM],
        out_specs=[VMEM] * count,
        out_shape=[jax.ShapeDtypeStruct(rest, source.dtype)] * count,
        compiler_params=pltpu.CompilerParams(vmem_limit_bytes=SMALL_VMEM),
        name="pick",
    )(index, source)


def pick_stacked_kernel(index_ref, in_ref, out_ref, sems):
    run_copies(
        [
            pltpu.make_async_copy(in_ref.at[index_ref[i]], out_ref.at[i], sems.at[i])
            for i in range(out_ref.shape[0])
        ]
    )


def pick_stacked(index, source):
    count, rest = index.shape[0], source.shape[1:]
    return pl.pallas_call(
        pick_stacked_kernel,
        in_specs=[SMEM, VMEM],
        out_specs=ANY,
        out_shape=jax.ShapeDtypeStruct((count,) + rest, source.dtype),
        scratch_shapes=[pltpu.SemaphoreType.DMA((count,))],
        compiler_params=pltpu.CompilerParams(vmem_limit_bytes=SMALL_VMEM),
        name="pick_stacked",
    )(index, source)


def place_q_kernel(index_ref, *refs):
    ins, out_ref, sems = refs[:-2], refs[-2], refs[-1]
    kv_heads, _, width = ins[0].shape

    def copy(source, s, h):
        return pltpu.make_async_copy(
            source.at[h], out_ref.at[s, :, pl.ds(h * width, width)], sems.at[s, h]
        )

    for s in range(out_ref.shape[0]):
        for i, source in enumerate(ins):

            @pl.when(index_ref[s] == i)
            def _():
                for h in range(kv_heads):
                    copy(source, s, h).start()

    for s in range(out_ref.shape[0]):
        for h in range(kv_heads):
            copy(ins[0], s, h).wait()


def place_q(index, sources):
    count = index.shape[0]
    kv_heads, block, width = sources[0].shape
    return pl.pallas_call(
        place_q_kernel,
        in_specs=[SMEM] + [VMEM] * len(sources),
        out_specs=ANY,
        out_shape=jax.ShapeDtypeStruct((count, block, kv_heads * width), BF16),
        scratch_shapes=[pltpu.SemaphoreType.DMA((count, kv_heads))],
        compiler_params=pltpu.CompilerParams(vmem_limit_bytes=SMALL_VMEM),
        name="place_q",
    )(index, *sources)


def place_kv_kernel(index_ref, in_ref, key_ref, value_ref, sems):
    copies = []
    for s in range(key_ref.shape[0]):
        for h in range(in_ref.shape[1]):
            for w, out_ref in enumerate((key_ref, value_ref)):
                copies.append(
                    pltpu.make_async_copy(
                        in_ref.at[index_ref[s], h, :, pl.ds(w * HEAD, HEAD)],
                        out_ref.at[s, :, pl.ds(h * HEAD, HEAD)],
                        sems.at[s, h, w],
                    )
                )
    run_copies(copies)


def place_kv(index, source):
    count = index.shape[0]
    _, kv_heads, block, _ = source.shape
    return pl.pallas_call(
        place_kv_kernel,
        in_specs=[SMEM, VMEM],
        out_specs=[ANY] * 2,
        out_shape=[jax.ShapeDtypeStruct((count, block, kv_heads * HEAD), BF16)] * 2,
        scratch_shapes=[pltpu.SemaphoreType.DMA((count, kv_heads, 2))],
        compiler_params=pltpu.CompilerParams(vmem_limit_bytes=SMALL_VMEM),
        name="place_kv",
    )(index, source)


def exchange(x, axis, groups=None):
    return lax.all_to_all(
        x, axis, split_axis=0, concat_axis=0, tiled=True, axis_index_groups=groups
    )


def on_device(
    queries, key_states, value_state_rows, segment_ids, output_grad, out_weight, destination
):
    rows, block, q_width = queries.shape
    kv_heads = key_states.shape[2] // HEAD
    units = rows * kv_heads
    n_ctx = lax.axis_size("ctx")
    groups = lax.axis_size("dp")
    pair = n_ctx // units
    ctx = lax.axis_index("ctx")
    tp = lax.axis_index("tp")
    group = lax.axis_index("dp")
    side = ctx % pair
    columns = [[z * pair + h for z in ORDER] for h in range(pair)]
    swap = [(z * pair + h, z * pair + 1 - h) for z in range(units) for h in range(pair)]

    other_grad = lax.ppermute(output_grad, "tp", [(0, 1), (1, 0)])

    own = pack(segment_ids, key_states, value_state_rows)
    own = exchange(own, "ctx", columns)
    other = lax.ppermute(own, "ctx", swap)

    def partner(g, i, sign):
        chips = groups // 2
        return (g // 2 + sign * (i // 2) + chips) % chips * 2 + (g % 2 + i) % 2

    steps = jnp.arange(groups, dtype=jnp.int32)
    dest = destination.reshape(groups, rows)
    own_targets = lax.dynamic_slice_in_dim(dest, group, 1, 0) // rows

    def row_for(targets):
        return jnp.sum(
            jnp.where(
                own_targets == targets[:, None],
                jnp.arange(rows, dtype=jnp.int32)[None, :],
                0,
            ),
            axis=1,
        )

    wanted = group * rows + jnp.arange(rows, dtype=jnp.int32)
    recv_index = jnp.sum(
        jnp.where(
            destination[None, :] == wanted[:, None],
            jnp.arange(groups * rows, dtype=jnp.int32)[None, :] // rows,
            0,
        ),
        axis=1,
    )
    recv_step = jnp.sum(
        jnp.where(recv_index[:, None] == partner(group, steps, -1)[None, :], steps, 0),
        axis=1,
    )
    send_index = row_for(steps)
    send_step = row_for(partner(group, steps, 1))

    index = tp[None].astype(jnp.int32)
    part, turned = project_own(output_grad, out_weight, index)
    q_and_grad = project_other(other_grad, turned, part, queries, kv_heads)
    q_and_grad = q_and_grad.reshape(units, block, q_and_grad.shape[3])
    q_and_grad = exchange(q_and_grad, "ctx", columns)

    dq, dkv_mine, dkv_theirs = attention(
        side[None].astype(jnp.int32), own, other, q_and_grad
    )

    dkv_back = lax.ppermute(dkv_theirs, "ctx", swap)
    dq = exchange(dq, "ctx", columns)
    dkv = (dkv_mine.astype(F32) + dkv_back.astype(F32)).astype(BF16)
    dkv, dq = lax.optimization_barrier((dkv, dq))
    dkv = exchange(dkv, "ctx", columns)

    def by_row(x):
        return x.reshape(rows, kv_heads, block, x.shape[2])

    sent = pick_rows(send_step, by_row(dq))
    got = [sent[0]]
    for i in range(1, groups):
        route = [(g, partner(g, i, 1)) for g in range(groups)]
        got.append(lax.ppermute(sent[i], "dp", route))
    dkv, *got = lax.optimization_barrier((dkv, *got))
    query_out = place_q(recv_step, got)
    dkv = exchange(pick_stacked(send_index, by_row(dkv)), "dp")
    key_out, value_out = place_kv(recv_index, dkv)
    return query_out, key_out, value_out


def solution(mesh):
    in_specs = (
        P("dp", "ctx", "tp"),
        P("dp", "ctx", "tp"),
        P("dp", "ctx", "tp"),
        P("dp", "ctx"),
        P("dp", "ctx", "tp"),
        P("tp", None),
        P(),
    )
    out_specs = (P("dp", "ctx", "tp"), P("dp", "ctx", "tp"), P("dp", "ctx", "tp"))
    return jax.shard_map(
        on_device, mesh=mesh, in_specs=in_specs, out_specs=out_specs, check_vma=False
    )
```

```python
import jax
import jax.numpy as jnp
from jax import lax
from jax.experimental import pallas as pl
from jax.experimental.pallas import tpu as pltpu
from jax.sharding import PartitionSpec as P

HEAD = 256
CAP = 50.0
SCALE = 0.0625
LOG2E = 1.4426950408889634
F32 = jnp.float32
BF16 = jnp.bfloat16
TILE = 16
ORDER = (0, 2, 4, 6, 1, 3, 5, 7)
SLOT = tuple(ORDER.index(z) for z in range(len(ORDER)))
SMALL_VMEM = 8 * 1024 * 1024
MEDIUM_VMEM = 14 * 1024 * 1024
LARGE_VMEM = 28 * 1024 * 1024


def dot(a, b, ca, cb):
    return lax.dot_general(a, b, (((ca,), (cb,)), ((), ())), preferred_element_type=F32)


VMEM = pl.BlockSpec(memory_space=pltpu.VMEM)
SMEM = pl.BlockSpec(memory_space=pltpu.SMEM)
ANY = pl.BlockSpec(memory_space=pl.ANY)


def load_half(index, weight_hbm, weight_ref, sems):
    half = weight_ref.shape[1]
    columns = pl.ds(pl.multiple_of(index * half, 128), half)
    parts = [slice(h, h + HEAD) for h in range(0, weight_ref.shape[0], HEAD)]
    copies = [
        pltpu.make_async_copy(weight_hbm.at[at, columns], weight_ref.at[at], sems.at[i])
        for i, at in enumerate(parts)
    ]
    for copy in copies:
        copy.start()
    for at, copy in zip(parts, copies):
        copy.wait()
        yield at


def own_half(tp, x_ref, weight_hbm, part_ref, weight_ref, sems):
    rows, block, half = x_ref.shape
    for at in load_half(tp, weight_hbm, weight_ref, sems):
        x = x_ref[...].reshape(rows * block, half)
        part_ref[:, at] = dot(x, weight_ref[at], 1, 1)


def begin_kernel(
    place_ref,
    seg_hbm,
    k_hbm,
    v_hbm,
    x_hbm,
    weight_hbm,
    out_ref,
    x_ref,
    part_ref,
    seg_ref,
    k_ref,
    v_ref,
    weight_ref,
    sems,
    weight_sems,
):
    rows, block, kv_width = k_ref.shape
    kv_heads = kv_width // HEAD
    pieces = block // TILE
    copies = [
        pltpu.make_async_copy(source, target, sems.at[i])
        for i, (source, target) in enumerate(
            ((seg_hbm, seg_ref), (k_hbm, k_ref), (v_hbm, v_ref), (x_hbm, x_ref))
        )
    ]
    for copy in copies:
        copy.start()
    copies[3].wait()

    @pl.when(place_ref[1] == 0)
    def _():
        own_half(place_ref[0], x_ref, weight_hbm, part_ref, weight_ref, weight_sems)

    copies[0].wait()
    place = lax.broadcasted_iota(jnp.int32, (TILE, block), 1)
    row = lax.broadcasted_iota(jnp.int32, (TILE, block), 0)
    lane = lax.broadcasted_iota(jnp.int32, (TILE, 128), 1)
    for r in range(rows):
        spread = jnp.broadcast_to(seg_ref[r : r + 1], (TILE, block)).astype(F32)
        columns = jnp.zeros((TILE, 128), F32)
        for j in range(pieces):
            column = jnp.sum(
                jnp.where(place == row + j * TILE, spread, 0.0), axis=1, keepdims=True
            )
            columns = jnp.where(lane == j, column, columns)
        for h in range(kv_heads):
            out_ref[r * kv_heads + h, :, pieces * 2 * HEAD :] = columns.astype(BF16)
    copies[1].wait()
    copies[2].wait()
    for r in range(rows):
        for h in range(kv_heads):
            u = r * kv_heads + h
            heads = slice(h * HEAD, (h + 1) * HEAD)
            for j in range(pieces):
                at = slice(j * TILE, (j + 1) * TILE)
                k_at = j * 2 * HEAD
                out_ref[u, :, k_at : k_at + HEAD] = k_ref[r, at, heads]
                out_ref[u, :, k_at + HEAD : k_at + 2 * HEAD] = v_ref[r, at, heads]


def in_hbm(*arrays):
    return [pltpu.with_memory_space_constraint(x, pltpu.HBM) for x in arrays]


def begin(place, seg, k, v, x, weight):
    rows, block, kv_width = k.shape
    kv_heads = kv_width // HEAD
    lanes = block // TILE * 2 * HEAD + 128
    width, half = weight.shape[0], x.shape[2]
    return pl.pallas_call(
        begin_kernel,
        in_specs=[SMEM] + [ANY] * 5,
        out_specs=[VMEM] * 3,
        out_shape=[
            pltpu.HBM((rows * kv_heads, TILE, lanes), BF16),
            jax.ShapeDtypeStruct(x.shape, BF16),
            jax.ShapeDtypeStruct((rows * block, width), F32),
        ],
        scratch_shapes=[
            pltpu.VMEM(seg.shape, jnp.int32),
            pltpu.VMEM(k.shape, BF16),
            pltpu.VMEM(v.shape, BF16),
            pltpu.VMEM((width, half), BF16),
            pltpu.SemaphoreType.DMA((4,)),
            pltpu.SemaphoreType.DMA((width // HEAD,)),
        ],
        compiler_params=pltpu.CompilerParams(vmem_limit_bytes=MEDIUM_VMEM),
        name="begin",
    )(place, *in_hbm(seg, k, v, x, weight))


def project_own_kernel(
    place_ref, x_ref, weight_hbm, part_ref, turned_ref, weight_ref, sems
):
    for at in load_half(1 - place_ref[0], weight_hbm, weight_ref, sems):
        turned_ref[:, at] = weight_ref[at].T

    @pl.when(place_ref[1] != 0)
    def _():
        own_half(place_ref[0], x_ref, weight_hbm, part_ref, weight_ref, sems)


def project_own(place, x, weight):
    rows, block, half = x.shape
    width = weight.shape[0]
    return pl.pallas_call(
        project_own_kernel,
        in_specs=[SMEM, VMEM, ANY],
        out_specs=[VMEM, VMEM],
        out_shape=[
            jax.ShapeDtypeStruct((rows * block, width), F32),
            jax.ShapeDtypeStruct((half, width), BF16),
        ],
        scratch_shapes=[
            pltpu.VMEM((width, half), BF16),
            pltpu.SemaphoreType.DMA((width // HEAD,)),
        ],
        compiler_params=pltpu.CompilerParams(vmem_limit_bytes=MEDIUM_VMEM),
        cost_estimate=pl.CostEstimate(
            flops=2 * rows * block * half * width,
            bytes_accessed=4 * half * width,
            transcendentals=0,
        ),
        name="project_own",
    )(place, x, *in_hbm(weight))


def other_half_kernel(place_ref, x_ref, q_ref, part_0, part_1, turned_ref, out_ref):
    rows, block, half = x_ref.shape
    kv_heads = out_ref.shape[1]
    width = turned_ref.shape[1] // kv_heads
    x = x_ref[...].reshape(rows * block, half)
    for h in range(kv_heads):
        at = slice(h * width, (h + 1) * width)
        out_ref[:, h, :, :width] = q_ref[:, :, at]
        part = jnp.where(place_ref[1] == 0, part_0[:, at], part_1[:, at])
        total = part + dot(x, turned_ref[:, at], 1, 0)
        out_ref[:, h, :, width:] = total.astype(BF16).reshape(rows, block, width)


def project_other(place, x, q, part_0, part_1, turned, kv_heads):
    rows, block, half = x.shape
    total = turned.shape[1]
    return pl.pallas_call(
        other_half_kernel,
        in_specs=[SMEM] + [VMEM] * 5,
        out_specs=VMEM,
        out_shape=pltpu.HBM((rows, kv_heads, block, 2 * total // kv_heads), BF16),
        compiler_params=pltpu.CompilerParams(vmem_limit_bytes=MEDIUM_VMEM),
        cost_estimate=pl.CostEstimate(
            flops=2 * rows * block * half * total,
            bytes_accessed=2 * half * total,
            transcendentals=0,
        ),
        name="project_other",
    )(place, x, q, part_0, part_1, turned)


def attention_kernel(
    side_ref, own_ref, other_ref, qd_ref, dq_ref, dkv_own, dkv_other, acc
):
    steps, block, width = dq_ref.shape
    per = 2
    lanes = per * block
    pieces = block // TILE
    side = side_ref[0]

    def gathered(ref, low, high, start):
        return jnp.concatenate(
            [
                ref[SLOT[z], :, start + j * 2 * HEAD : start + j * 2 * HEAD + HEAD]
                for z in range(low, high)
                for j in range(pieces)
            ],
            axis=0,
        )

    def ids(ref, low, high):
        return jnp.concatenate(
            [
                ref[SLOT[z], :, pieces * 2 * HEAD :].astype(F32)[:, j : j + 1]
                for z in range(low, high)
                for j in range(pieces)
            ],
            axis=0,
        )

    def positions(shape, axis, low, which):
        n = lax.broadcasted_iota(jnp.int32, shape, axis)
        return 2 * n - (n & (block - 1)) + (per * block * low + block * which)

    diagonal = lax.broadcasted_iota(
        jnp.int32, (lanes, lanes), 0
    ) == lax.broadcasted_iota(jnp.int32, (lanes, lanes), 1)

    def scores(z):
        low, high = max(0, z - 4), z + per
        qd = jnp.concatenate([qd_ref[SLOT[i]] for i in range(z, high)], axis=0)
        q = jnp.concatenate([qd[:, :HEAD], qd[:, HEAD:width]], axis=0)
        do = jnp.concatenate(
            [qd[:, width : width + HEAD], qd[:, width + HEAD :]], axis=0
        )
        seg_q = ids(own_ref, z, high)
        seg_q = jnp.sum(jnp.where(diagonal, seg_q, 0.0), axis=0, keepdims=True)
        pos_q = positions((1, lanes), 1, z, side)
        parts = []
        total = 0.0
        weighted = 0.0
        for which, ref in enumerate((own_ref, other_ref)):
            for start, stop in ((low, z), (z, high)):
                if start == stop:
                    continue
                k = gathered(ref, start, stop, 0)
                v = gathered(ref, start, stop, HEAD)
                allowed = ids(ref, start, stop) == seg_q
                if start == z:
                    key_side = side if which == 0 else 1 - side
                    pos_k = positions((lanes, lanes), 0, z, key_side)
                    allowed &= pos_k <= pos_q
                allowed = jnp.concatenate([allowed, allowed], axis=1)
                t = jnp.tanh(dot(k, q, 1, 1) * (SCALE / CAP))
                e = jnp.where(allowed, jnp.exp2(t * (CAP * LOG2E)), 0.0)
                dp = dot(v, do, 1, 1)
                total += jnp.sum(e, axis=0, keepdims=True)
                weighted += jnp.sum(e * dp, axis=0, keepdims=True)
                parts.append((which, start, stop, k, t, e, dp))
        return z, q, do, parts, total, weighted

    def gradients(z, q, do, parts, total, weighted):
        inverse = 1.0 / total
        delta = weighted * inverse
        dq = 0.0
        for which, start, stop, k, t, e, dp in parts:
            prob = e * inverse
            ds = (prob * (dp - delta) * (1.0 - t * t)).astype(BF16)
            at = slice(start * block, stop * block)
            dk, dv = dot(ds, q, 1, 0), dot(prob.astype(BF16), do, 1, 0)
            if z == start:
                acc[which, at, :HEAD] = dk
                acc[which, at, HEAD:] = dv
            else:
                acc[which, at, :HEAD] += dk
                acc[which, at, HEAD:] += dv
            dq += dot(ds, k, 0, 0)
        dq = (dq * SCALE).astype(BF16)
        for i in range(per):
            at = slice(i * block, (i + 1) * block)
            dq_ref[SLOT[z + i], :, :HEAD] = dq[:lanes][at]
            dq_ref[SLOT[z + i], :, HEAD:] = dq[lanes:][at]

    held = None
    for z in range(0, steps, per):
        ready = scores(z)
        if held is not None:
            gradients(*held)
        held = ready
    gradients(*held)
    for z in range(steps):
        at = slice(z * block, (z + 1) * block)
        for which, out_ref in enumerate((dkv_own, dkv_other)):
            out_ref[SLOT[z], :, :HEAD] = (acc[which, at, :HEAD] * SCALE).astype(BF16)
            out_ref[SLOT[z], :, HEAD:] = acc[which, at, HEAD:].astype(BF16)


def attention(side, own, other, q_and_grad):
    steps, block, width = q_and_grad.shape
    width //= 2
    return pl.pallas_call(
        attention_kernel,
        in_specs=[SMEM] + [VMEM] * 3,
        out_specs=[VMEM] * 3,
        out_shape=[
            pltpu.HBM((steps, block, width), BF16),
            pltpu.VMEM((steps, block, width), BF16),
            pltpu.VMEM((steps, block, width), BF16),
        ],
        scratch_shapes=[pltpu.VMEM((2, steps * block, width), F32)],
        compiler_params=pltpu.CompilerParams(vmem_limit_bytes=LARGE_VMEM),
        cost_estimate=pl.CostEstimate(
            flops=3 * 10**9, bytes_accessed=6 * 2**20, transcendentals=1200000
        ),
        name="attend",
    )(side, own, other, q_and_grad)


def run_copies(copies):
    for copy in copies:
        copy.start()
    for copy in copies:
        copy.wait()


def pick_kernel(index_ref, in_ref, *outs):
    for i, out in enumerate(outs):
        out[...] = in_ref[index_ref[i]]


def pick_rows(index, source):
    count, rest = index.shape[0], source.shape[1:]
    return pl.pallas_call(
        pick_kernel,
        in_specs=[SMEM, VMEM],
        out_specs=[VMEM] * count,
        out_shape=[jax.ShapeDtypeStruct(rest, source.dtype)] * count,
        compiler_params=pltpu.CompilerParams(vmem_limit_bytes=SMALL_VMEM),
        name="pick",
    )(index, source)


def pick_stacked_kernel(index_ref, in_ref, out_ref, sems):
    run_copies(
        [
            pltpu.make_async_copy(in_ref.at[index_ref[i]], out_ref.at[i], sems.at[i])
            for i in range(out_ref.shape[0])
        ]
    )


def pick_stacked(index, source):
    count, rest = index.shape[0], source.shape[1:]
    return pl.pallas_call(
        pick_stacked_kernel,
        in_specs=[SMEM, VMEM],
        out_specs=ANY,
        out_shape=jax.ShapeDtypeStruct((count,) + rest, source.dtype),
        scratch_shapes=[pltpu.SemaphoreType.DMA((count,))],
        compiler_params=pltpu.CompilerParams(vmem_limit_bytes=SMALL_VMEM),
        name="pick_stacked",
    )(index, source)


def place_q_kernel(index_ref, *refs):
    ins, out_ref, sems = refs[:-2], refs[-2], refs[-1]
    kv_heads, _, width = ins[0].shape

    def copy(source, s, h):
        return pltpu.make_async_copy(
            source.at[h], out_ref.at[s, :, pl.ds(h * width, width)], sems.at[s, h]
        )

    for s in range(out_ref.shape[0]):
        for i, source in enumerate(ins):

            @pl.when(index_ref[s] == i)
            def _():
                for h in range(kv_heads):
                    copy(source, s, h).start()

    for s in range(out_ref.shape[0]):
        for h in range(kv_heads):
            copy(ins[0], s, h).wait()


def place_q(index, sources):
    count = index.shape[0]
    kv_heads, block, width = sources[0].shape
    return pl.pallas_call(
        place_q_kernel,
        in_specs=[SMEM] + [VMEM] * len(sources),
        out_specs=ANY,
        out_shape=jax.ShapeDtypeStruct((count, block, kv_heads * width), BF16),
        scratch_shapes=[pltpu.SemaphoreType.DMA((count, kv_heads))],
        compiler_params=pltpu.CompilerParams(vmem_limit_bytes=SMALL_VMEM),
        name="place_q",
    )(index, *sources)


def place_kv_kernel(index_ref, in_ref, key_ref, value_ref, sems):
    copies = []
    for s in range(key_ref.shape[0]):
        for h in range(in_ref.shape[1]):
            for w, out_ref in enumerate((key_ref, value_ref)):
                copies.append(
                    pltpu.make_async_copy(
                        in_ref.at[index_ref[s], h, :, pl.ds(w * HEAD, HEAD)],
                        out_ref.at[s, :, pl.ds(h * HEAD, HEAD)],
                        sems.at[s, h, w],
                    )
                )
    run_copies(copies)


def place_kv(index, source):
    count = index.shape[0]
    _, kv_heads, block, _ = source.shape
    return pl.pallas_call(
        place_kv_kernel,
        in_specs=[SMEM, VMEM],
        out_specs=[ANY] * 2,
        out_shape=[jax.ShapeDtypeStruct((count, block, kv_heads * HEAD), BF16)] * 2,
        scratch_shapes=[pltpu.SemaphoreType.DMA((count, kv_heads, 2))],
        compiler_params=pltpu.CompilerParams(vmem_limit_bytes=SMALL_VMEM),
        name="place_kv",
    )(index, source)


def exchange(x, axis, groups=None):
    return lax.all_to_all(
        x, axis, split_axis=0, concat_axis=0, tiled=True, axis_index_groups=groups
    )


def on_device(
    queries, key_states, value_state_rows, segment_ids, output_grad, out_weight, destination
):
    rows, block, q_width = queries.shape
    kv_heads = key_states.shape[2] // HEAD
    units = rows * kv_heads
    n_ctx = lax.axis_size("ctx")
    groups = lax.axis_size("dp")
    pair = n_ctx // units
    ctx = lax.axis_index("ctx")
    tp = lax.axis_index("tp")
    group = lax.axis_index("dp")
    side = ctx % pair
    columns = [[z * pair + h for z in ORDER] for h in range(pair)]
    swap = [(z * pair + h, z * pair + 1 - h) for z in range(units) for h in range(pair)]

    place = jnp.stack([tp, group % 2]).astype(jnp.int32)
    own, grad, part_0 = begin(
        place, segment_ids, key_states, value_state_rows, output_grad, out_weight
    )
    other_grad = lax.ppermute(grad, "tp", [(0, 1), (1, 0)])
    own = exchange(own, "ctx", columns)
    other = lax.ppermute(own, "ctx", swap)

    def partner(g, i, sign):
        chips = groups // 2
        return (g // 2 + sign * (i // 2) + chips) % chips * 2 + (g % 2 + i) % 2

    steps = jnp.arange(groups, dtype=jnp.int32)
    dest = destination.reshape(groups, rows)
    own_targets = lax.dynamic_slice_in_dim(dest, group, 1, 0) // rows

    def row_for(targets):
        return jnp.sum(
            jnp.where(
                own_targets == targets[:, None],
                jnp.arange(rows, dtype=jnp.int32)[None, :],
                0,
            ),
            axis=1,
        )

    wanted = group * rows + jnp.arange(rows, dtype=jnp.int32)
    recv_index = jnp.sum(
        jnp.where(
            destination[None, :] == wanted[:, None],
            jnp.arange(groups * rows, dtype=jnp.int32)[None, :] // rows,
            0,
        ),
        axis=1,
    )
    recv_step = jnp.sum(
        jnp.where(recv_index[:, None] == partner(group, steps, -1)[None, :], steps, 0),
        axis=1,
    )
    send_index = row_for(steps)
    send_step = row_for(partner(group, steps, 1))

    part_1, turned = project_own(place, grad, out_weight)
    q_and_grad = project_other(
        place, other_grad, queries, part_0, part_1, turned, kv_heads
    )
    q_and_grad = q_and_grad.reshape(units, block, q_and_grad.shape[3])
    q_and_grad = exchange(q_and_grad, "ctx", columns)

    dq, dkv_mine, dkv_theirs = attention(
        side[None].astype(jnp.int32), own, other, q_and_grad
    )

    dkv_back = lax.ppermute(dkv_theirs, "ctx", swap)
    dq = exchange(dq, "ctx", columns)
    dkv = (dkv_mine.astype(F32) + dkv_back.astype(F32)).astype(BF16)
    dkv, dq = lax.optimization_barrier((dkv, dq))
    dkv = exchange(dkv, "ctx", columns)

    def by_row(x):
        return x.reshape(rows, kv_heads, block, x.shape[2])

    sent = pick_rows(send_step, by_row(dq))
    got = [sent[0]]
    for i in range(1, groups):
        route = [(g, partner(g, i, 1)) for g in range(groups)]
        got.append(lax.ppermute(sent[i], "dp", route))
    dkv, *got = lax.optimization_barrier((dkv, *got))
    query_out = place_q(recv_step, got)
    dkv = exchange(pick_stacked(send_index, by_row(dkv)), "dp")
    key_out, value_out = place_kv(recv_index, dkv)
    return query_out, key_out, value_out


def solution(mesh):
    in_specs = (
        P("dp", "ctx", "tp"),
        P("dp", "ctx", "tp"),
        P("dp", "ctx", "tp"),
        P("dp", "ctx"),
        P("dp", "ctx", "tp"),
        P("tp", None),
        P(),
    )
    out_specs = (P("dp", "ctx", "tp"), P("dp", "ctx", "tp"), P("dp", "ctx", "tp"))
    return jax.shard_map(
        on_device, mesh=mesh, in_specs=in_specs, out_specs=out_specs, check_vma=False
    )
```

```python
import jax
import jax.numpy as jnp
from jax import lax
from jax.experimental import pallas as pl
from jax.experimental.pallas import tpu as pltpu
from jax.sharding import PartitionSpec as P

HEAD = 256
CAP = 50.0
SCALE = 0.0625
LOG2E = 1.4426950408889634
F32 = jnp.float32
BF16 = jnp.bfloat16
TILE = 16
ORDER = (0, 2, 4, 6, 1, 3, 5, 7)
SLOT = tuple(ORDER.index(z) for z in range(len(ORDER)))
SMALL_VMEM = 8 * 1024 * 1024
MEDIUM_VMEM = 14 * 1024 * 1024
LARGE_VMEM = 28 * 1024 * 1024


def dot(a, b, ca, cb):
    return lax.dot_general(a, b, (((ca,), (cb,)), ((), ())), preferred_element_type=F32)


VMEM = pl.BlockSpec(memory_space=pltpu.VMEM)
SMEM = pl.BlockSpec(memory_space=pltpu.SMEM)
ANY = pl.BlockSpec(memory_space=pl.ANY)


def load_half(index, weight_hbm, weight_ref, sems):
    half = weight_ref.shape[1]
    columns = pl.ds(pl.multiple_of(index * half, 128), half)
    parts = [slice(h, h + HEAD) for h in range(0, weight_ref.shape[0], HEAD)]
    copies = [
        pltpu.make_async_copy(weight_hbm.at[at, columns], weight_ref.at[at], sems.at[i])
        for i, at in enumerate(parts)
    ]
    for copy in copies:
        copy.start()
    for at, copy in zip(parts, copies):
        copy.wait()
        yield at


def own_half(tp, x_ref, weight_hbm, part_ref, weight_ref, sems):
    rows, block, half = x_ref.shape
    for at in load_half(tp, weight_hbm, weight_ref, sems):
        x = x_ref[...].reshape(rows * block, half)
        part_ref[:, at] = dot(x, weight_ref[at], 1, 1)


def on_core():
    return lax.rem(lax.axis_index("dp"), 2)


def begin_kernel(
    seg_hbm,
    k_hbm,
    v_hbm,
    x_hbm,
    weight_hbm,
    out_ref,
    x_ref,
    part_ref,
    seg_ref,
    k_ref,
    v_ref,
    weight_ref,
    sems,
    weight_sems,
):
    rows, block, kv_width = k_ref.shape
    kv_heads = kv_width // HEAD
    pieces = block // TILE
    copies = [
        pltpu.make_async_copy(source, target, sems.at[i])
        for i, (source, target) in enumerate(
            ((seg_hbm, seg_ref), (k_hbm, k_ref), (v_hbm, v_ref), (x_hbm, x_ref))
        )
    ]
    for copy in copies:
        copy.start()
    copies[3].wait()

    @pl.when(on_core() == 0)
    def _():
        own_half(lax.axis_index("tp"), x_ref, weight_hbm, part_ref, weight_ref, weight_sems)

    copies[0].wait()
    place = lax.broadcasted_iota(jnp.int32, (TILE, block), 1)
    row = lax.broadcasted_iota(jnp.int32, (TILE, block), 0)
    lane = lax.broadcasted_iota(jnp.int32, (TILE, 128), 1)
    for r in range(rows):
        spread = jnp.broadcast_to(seg_ref[r : r + 1], (TILE, block)).astype(F32)
        columns = jnp.zeros((TILE, 128), F32)
        for j in range(pieces):
            column = jnp.sum(
                jnp.where(place == row + j * TILE, spread, 0.0), axis=1, keepdims=True
            )
            columns = jnp.where(lane == j, column, columns)
        for h in range(kv_heads):
            out_ref[r * kv_heads + h, :, pieces * 2 * HEAD :] = columns.astype(BF16)
    copies[1].wait()
    copies[2].wait()
    for r in range(rows):
        for h in range(kv_heads):
            u = r * kv_heads + h
            heads = slice(h * HEAD, (h + 1) * HEAD)
            for j in range(pieces):
                at = slice(j * TILE, (j + 1) * TILE)
                k_at = j * 2 * HEAD
                out_ref[u, :, k_at : k_at + HEAD] = k_ref[r, at, heads]
                out_ref[u, :, k_at + HEAD : k_at + 2 * HEAD] = v_ref[r, at, heads]


def in_hbm(*arrays):
    return [pltpu.with_memory_space_constraint(x, pltpu.HBM) for x in arrays]


def begin(seg, k, v, x, weight):
    rows, block, kv_width = k.shape
    kv_heads = kv_width // HEAD
    lanes = block // TILE * 2 * HEAD + 128
    width, half = weight.shape[0], x.shape[2]
    return pl.pallas_call(
        begin_kernel,
        in_specs=[ANY] * 5,
        out_specs=[VMEM] * 3,
        out_shape=[
            pltpu.HBM((rows * kv_heads, TILE, lanes), BF16),
            jax.ShapeDtypeStruct(x.shape, BF16),
            jax.ShapeDtypeStruct((rows * block, width), F32),
        ],
        scratch_shapes=[
            pltpu.VMEM(seg.shape, jnp.int32),
            pltpu.VMEM(k.shape, BF16),
            pltpu.VMEM(v.shape, BF16),
            pltpu.VMEM((width, half), BF16),
            pltpu.SemaphoreType.DMA((4,)),
            pltpu.SemaphoreType.DMA((width // HEAD,)),
        ],
        compiler_params=pltpu.CompilerParams(vmem_limit_bytes=MEDIUM_VMEM),
        name="begin",
    )(*in_hbm(seg, k, v, x, weight))


def project_own_kernel(
    x_ref, weight_hbm, part_ref, turned_ref, weight_ref, sems
):
    for at in load_half(1 - lax.axis_index("tp"), weight_hbm, weight_ref, sems):
        turned_ref[:, at] = weight_ref[at].T

    @pl.when(on_core() != 0)
    def _():
        own_half(lax.axis_index("tp"), x_ref, weight_hbm, part_ref, weight_ref, sems)


def project_own(x, weight):
    rows, block, half = x.shape
    width = weight.shape[0]
    return pl.pallas_call(
        project_own_kernel,
        in_specs=[VMEM, ANY],
        out_specs=[VMEM, VMEM],
        out_shape=[
            jax.ShapeDtypeStruct((rows * block, width), F32),
            jax.ShapeDtypeStruct((half, width), BF16),
        ],
        scratch_shapes=[
            pltpu.VMEM((width, half), BF16),
            pltpu.SemaphoreType.DMA((width // HEAD,)),
        ],
        compiler_params=pltpu.CompilerParams(vmem_limit_bytes=MEDIUM_VMEM),
        cost_estimate=pl.CostEstimate(
            flops=2 * rows * block * half * width,
            bytes_accessed=4 * half * width,
            transcendentals=0,
        ),
        name="project_own",
    )(x, *in_hbm(weight))


def other_half_kernel(x_ref, q_ref, part_0, part_1, turned_ref, out_ref):
    rows, block, half = x_ref.shape
    kv_heads = out_ref.shape[1]
    width = turned_ref.shape[1] // kv_heads
    x = x_ref[...].reshape(rows * block, half)
    for h in range(kv_heads):
        at = slice(h * width, (h + 1) * width)
        out_ref[:, h, :, :width] = q_ref[:, :, at]
        part = jnp.where(on_core() == 0, part_0[:, at], part_1[:, at])
        total = part + dot(x, turned_ref[:, at], 1, 0)
        out_ref[:, h, :, width:] = total.astype(BF16).reshape(rows, block, width)


def project_other(x, q, part_0, part_1, turned, kv_heads):
    rows, block, half = x.shape
    total = turned.shape[1]
    return pl.pallas_call(
        other_half_kernel,
        in_specs=[VMEM] * 5,
        out_specs=VMEM,
        out_shape=pltpu.HBM((rows, kv_heads, block, 2 * total // kv_heads), BF16),
        compiler_params=pltpu.CompilerParams(vmem_limit_bytes=MEDIUM_VMEM),
        cost_estimate=pl.CostEstimate(
            flops=2 * rows * block * half * total,
            bytes_accessed=2 * half * total,
            transcendentals=0,
        ),
        name="project_other",
    )(x, q, part_0, part_1, turned)


def attention_kernel(
    own_ref,
    other_ref,
    qd_ref,
    dq_hbm,
    dkv_own,
    dkv_other,
    acc,
    dq_ref,
    sems,
):
    steps, block, width = dq_ref.shape
    per = 2
    lanes = per * block
    pieces = block // TILE
    side = lax.rem(lax.axis_index("ctx"), 2)

    def gathered(ref, low, high, start):
        return jnp.concatenate(
            [
                ref[SLOT[z], :, start + j * 2 * HEAD : start + j * 2 * HEAD + HEAD]
                for z in range(low, high)
                for j in range(pieces)
            ],
            axis=0,
        )

    def ids(ref, low, high):
        return jnp.concatenate(
            [
                ref[SLOT[z], :, pieces * 2 * HEAD :].astype(F32)[:, j : j + 1]
                for z in range(low, high)
                for j in range(pieces)
            ],
            axis=0,
        )

    def positions(shape, axis, low, which):
        n = lax.broadcasted_iota(jnp.int32, shape, axis)
        return 2 * n - (n & (block - 1)) + (per * block * low + block * which)

    diagonal = lax.broadcasted_iota(
        jnp.int32, (lanes, lanes), 0
    ) == lax.broadcasted_iota(jnp.int32, (lanes, lanes), 1)

    def scores(z):
        low, high = max(0, z - 4), z + per
        qd = jnp.concatenate([qd_ref[SLOT[i]] for i in range(z, high)], axis=0)
        q = jnp.concatenate([qd[:, :HEAD], qd[:, HEAD:width]], axis=0)
        do = jnp.concatenate(
            [qd[:, width : width + HEAD], qd[:, width + HEAD :]], axis=0
        )
        seg_q = ids(own_ref, z, high)
        seg_q = jnp.sum(jnp.where(diagonal, seg_q, 0.0), axis=0, keepdims=True)
        pos_q = positions((1, lanes), 1, z, side)
        parts = []
        total = 0.0
        weighted = 0.0
        for which, ref in enumerate((own_ref, other_ref)):
            for start, stop in ((low, z), (z, high)):
                if start == stop:
                    continue
                k = gathered(ref, start, stop, 0)
                v = gathered(ref, start, stop, HEAD)
                allowed = ids(ref, start, stop) == seg_q
                if start == z:
                    key_side = side if which == 0 else 1 - side
                    pos_k = positions((lanes, lanes), 0, z, key_side)
                    allowed &= pos_k <= pos_q
                allowed = jnp.concatenate([allowed, allowed], axis=1)
                t = jnp.tanh(dot(k, q, 1, 1) * (SCALE / CAP))
                e = jnp.where(allowed, jnp.exp2(t * (CAP * LOG2E)), 0.0)
                dp = dot(v, do, 1, 1)
                total += jnp.sum(e, axis=0, keepdims=True)
                weighted += jnp.sum(e * dp, axis=0, keepdims=True)
                parts.append((which, start, stop, k, t, e, dp))
        return z, q, do, parts, total, weighted

    def gradients(z, q, do, parts, total, weighted):
        inverse = 1.0 / total
        delta = weighted * inverse
        dq = 0.0
        for which, start, stop, k, t, e, dp in parts:
            prob = e * inverse
            ds = (prob * (dp - delta) * (1.0 - t * t)).astype(BF16)
            at = slice(start * block, stop * block)
            dk, dv = dot(ds, q, 1, 0), dot(prob.astype(BF16), do, 1, 0)
            if z == start:
                acc[which, at, :HEAD] = dk
                acc[which, at, HEAD:] = dv
            else:
                acc[which, at, :HEAD] += dk
                acc[which, at, HEAD:] += dv
            dq += dot(ds, k, 0, 0)
        dq = (dq * SCALE).astype(BF16)
        for i in range(per):
            at = slice(i * block, (i + 1) * block)
            slot = SLOT[z + i]
            dq_ref[slot, :, :HEAD] = dq[:lanes][at]
            dq_ref[slot, :, HEAD:] = dq[lanes:][at]
            copies.append(
                pltpu.make_async_copy(dq_ref.at[slot], dq_hbm.at[slot], sems.at[slot])
            )
            copies[-1].start()

    held = None
    copies = []
    for z in range(0, steps, per):
        ready = scores(z)
        if held is not None:
            gradients(*held)
        held = ready
    gradients(*held)
    for z in range(steps):
        at = slice(z * block, (z + 1) * block)
        for which, out_ref in enumerate((dkv_own, dkv_other)):
            out_ref[SLOT[z], :, :HEAD] = (acc[which, at, :HEAD] * SCALE).astype(BF16)
            out_ref[SLOT[z], :, HEAD:] = acc[which, at, HEAD:].astype(BF16)
    for copy in copies:
        copy.wait()


def attention(own, other, q_and_grad):
    steps, block, width = q_and_grad.shape
    width //= 2
    return pl.pallas_call(
        attention_kernel,
        in_specs=[VMEM] * 3,
        out_specs=[ANY, VMEM, VMEM],
        out_shape=[
            pltpu.HBM((steps, block, width), BF16),
            pltpu.VMEM((steps, block, width), BF16),
            pltpu.VMEM((steps, block, width), BF16),
        ],
        scratch_shapes=[
            pltpu.VMEM((2, steps * block, width), F32),
            pltpu.VMEM((steps, block, width), BF16),
            pltpu.SemaphoreType.DMA((steps,)),
        ],
        compiler_params=pltpu.CompilerParams(vmem_limit_bytes=LARGE_VMEM),
        cost_estimate=pl.CostEstimate(
            flops=3 * 10**9, bytes_accessed=6 * 2**20, transcendentals=1200000
        ),
        name="attend",
    )(own, other, q_and_grad)


def run_copies(copies):
    for copy in copies:
        copy.start()
    for copy in copies:
        copy.wait()


def pick_kernel(index_ref, in_ref, *outs):
    for i, out in enumerate(outs):

        @pl.when(index_ref[i] >= 0)
        def _():
            out[...] = in_ref[index_ref[i]]


def pick_rows(index, source):
    count, rest = index.shape[0], source.shape[1:]
    return pl.pallas_call(
        pick_kernel,
        in_specs=[SMEM, VMEM],
        out_specs=[VMEM] * count,
        out_shape=[jax.ShapeDtypeStruct(rest, source.dtype)] * count,
        compiler_params=pltpu.CompilerParams(vmem_limit_bytes=SMALL_VMEM),
        name="pick",
    )(index, source)


def pick_stacked_kernel(index_ref, in_ref, out_ref, sems):
    def each(act):
        for i in range(out_ref.shape[0]):

            @pl.when(index_ref[i] >= 0)
            def _():
                act(
                    pltpu.make_async_copy(
                        in_ref.at[index_ref[i]], out_ref.at[i], sems.at[i]
                    )
                )

    each(lambda copy: copy.start())
    each(lambda copy: copy.wait())


def pick_stacked(index, source):
    count, rest = index.shape[0], source.shape[1:]
    return pl.pallas_call(
        pick_stacked_kernel,
        in_specs=[SMEM, VMEM],
        out_specs=ANY,
        out_shape=jax.ShapeDtypeStruct((count,) + rest, source.dtype),
        scratch_shapes=[pltpu.SemaphoreType.DMA((count,))],
        compiler_params=pltpu.CompilerParams(vmem_limit_bytes=SMALL_VMEM),
        name="pick_stacked",
    )(index, source)


def place_q_kernel(index_ref, *refs):
    ins, out_ref, sems = refs[:-2], refs[-2], refs[-1]
    kv_heads, _, width = ins[0].shape

    def copy(source, s, h):
        return pltpu.make_async_copy(
            source.at[h], out_ref.at[s, :, pl.ds(h * width, width)], sems.at[s, h]
        )

    for s in range(out_ref.shape[0]):
        for i, source in enumerate(ins):

            @pl.when(index_ref[s] == i)
            def _():
                for h in range(kv_heads):
                    copy(source, s, h).start()

    for s in range(out_ref.shape[0]):
        for h in range(kv_heads):
            copy(ins[0], s, h).wait()


def place_q(index, sources):
    count = index.shape[0]
    kv_heads, block, width = sources[0].shape
    return pl.pallas_call(
        place_q_kernel,
        in_specs=[SMEM] + [VMEM] * len(sources),
        out_specs=ANY,
        out_shape=jax.ShapeDtypeStruct((count, block, kv_heads * width), BF16),
        scratch_shapes=[pltpu.SemaphoreType.DMA((count, kv_heads))],
        compiler_params=pltpu.CompilerParams(vmem_limit_bytes=SMALL_VMEM),
        name="place_q",
    )(index, *sources)


def place_kv_kernel(index_ref, in_ref, key_ref, value_ref, sems):
    copies = []
    for s in range(key_ref.shape[0]):
        for h in range(in_ref.shape[1]):
            for w, out_ref in enumerate((key_ref, value_ref)):
                copies.append(
                    pltpu.make_async_copy(
                        in_ref.at[index_ref[s], h, :, pl.ds(w * HEAD, HEAD)],
                        out_ref.at[s, :, pl.ds(h * HEAD, HEAD)],
                        sems.at[s, h, w],
                    )
                )
    run_copies(copies)


def place_kv(index, source):
    count = index.shape[0]
    _, kv_heads, block, _ = source.shape
    return pl.pallas_call(
        place_kv_kernel,
        in_specs=[SMEM, VMEM],
        out_specs=[ANY] * 2,
        out_shape=[jax.ShapeDtypeStruct((count, block, kv_heads * HEAD), BF16)] * 2,
        scratch_shapes=[pltpu.SemaphoreType.DMA((count, kv_heads, 2))],
        compiler_params=pltpu.CompilerParams(vmem_limit_bytes=SMALL_VMEM),
        name="place_kv",
    )(index, source)


def exchange(x, axis, groups=None):
    return lax.all_to_all(
        x, axis, split_axis=0, concat_axis=0, tiled=True, axis_index_groups=groups
    )


def on_device(
    queries, key_states, value_state_rows, segment_ids, output_grad, out_weight, destination
):
    rows, block, q_width = queries.shape
    kv_heads = key_states.shape[2] // HEAD
    units = rows * kv_heads
    n_ctx = lax.axis_size("ctx")
    groups = lax.axis_size("dp")
    pair = n_ctx // units
    ctx = lax.axis_index("ctx")
    group = lax.axis_index("dp")
    side = ctx % pair
    columns = [[z * pair + h for z in ORDER] for h in range(pair)]
    swap = [(z * pair + h, z * pair + 1 - h) for z in range(units) for h in range(pair)]

    own, grad, part_0 = begin(
        segment_ids, key_states, value_state_rows, output_grad, out_weight
    )
    other_grad = lax.ppermute(grad, "tp", [(0, 1), (1, 0)])
    own = exchange(own, "ctx", columns)
    other = lax.ppermute(own, "ctx", swap)

    def partner(g, i, sign):
        chips = groups // 2
        return (g // 2 + sign * (i // 2) + chips) % chips * 2 + (g % 2 + i) % 2

    steps = jnp.arange(groups, dtype=jnp.int32)
    dest = destination.reshape(groups, rows)
    own_targets = lax.dynamic_slice_in_dim(dest, group, 1, 0) // rows

    def row_for(targets):
        return (
            jnp.sum(
                jnp.where(
                    own_targets == targets[:, None],
                    jnp.arange(1, rows + 1, dtype=jnp.int32)[None, :],
                    0,
                ),
                axis=1,
            )
            - 1
        )

    wanted = group * rows + jnp.arange(rows, dtype=jnp.int32)
    recv_index = jnp.sum(
        jnp.where(
            destination[None, :] == wanted[:, None],
            jnp.arange(groups * rows, dtype=jnp.int32)[None, :] // rows,
            0,
        ),
        axis=1,
    )
    recv_step = jnp.sum(
        jnp.where(recv_index[:, None] == partner(group, steps, -1)[None, :], steps, 0),
        axis=1,
    )
    send_index = row_for(steps)
    send_step = row_for(partner(group, steps, 1))

    part_1, turned = project_own(grad, out_weight)
    q_and_grad = project_other(
        other_grad, queries, part_0, part_1, turned, kv_heads
    )
    q_and_grad = q_and_grad.reshape(units, block, q_and_grad.shape[3])
    q_and_grad = exchange(q_and_grad, "ctx", columns)

    dq, dkv_mine, dkv_theirs = attention(own, other, q_and_grad)

    dkv_back = lax.ppermute(dkv_theirs, "ctx", swap)
    dq = exchange(dq, "ctx", columns)
    dkv = (dkv_mine.astype(F32) + dkv_back.astype(F32)).astype(BF16)
    dkv, dq = lax.optimization_barrier((dkv, dq))
    dkv = exchange(dkv, "ctx", columns)

    def by_row(x):
        return x.reshape(rows, kv_heads, block, x.shape[2])

    sent = pick_rows(send_step, by_row(dq))
    got = [sent[0]]
    for i in range(1, groups):
        route = [(g, partner(g, i, 1)) for g in range(groups)]
        got.append(lax.ppermute(sent[i], "dp", route))
    dkv, *got = lax.optimization_barrier((dkv, *got))
    query_out = place_q(recv_step, got)
    dkv = exchange(pick_stacked(send_index, by_row(dkv)), "dp")
    key_out, value_out = place_kv(recv_index, dkv)
    return query_out, key_out, value_out


def solution(mesh):
    in_specs = (
        P("dp", "ctx", "tp"),
        P("dp", "ctx", "tp"),
        P("dp", "ctx", "tp"),
        P("dp", "ctx"),
        P("dp", "ctx", "tp"),
        P("tp", None),
        P(),
    )
    out_specs = (P("dp", "ctx", "tp"), P("dp", "ctx", "tp"), P("dp", "ctx", "tp"))
    return jax.shard_map(
        on_device, mesh=mesh, in_specs=in_specs, out_specs=out_specs, check_vma=False
    )
```

```python
import jax
import jax.numpy as jnp
from jax import lax
from jax.experimental import pallas as pl
from jax.experimental.pallas import tpu as pltpu
from jax.sharding import PartitionSpec as P

HEAD = 256
CAP = 50.0
SCALE = 0.0625
LOG2E = 1.4426950408889634
F32 = jnp.float32
BF16 = jnp.bfloat16
TILE = 16
ORDER = (0, 2, 4, 6, 1, 3, 5, 7)
SLOT = tuple(ORDER.index(z) for z in range(len(ORDER)))
SMALL_VMEM = 8 * 1024 * 1024
MEDIUM_VMEM = 14 * 1024 * 1024
LARGE_VMEM = 28 * 1024 * 1024


def dot(a, b, ca, cb):
    return lax.dot_general(a, b, (((ca,), (cb,)), ((), ())), preferred_element_type=F32)


VMEM = pl.BlockSpec(memory_space=pltpu.VMEM)
SMEM = pl.BlockSpec(memory_space=pltpu.SMEM)
ANY = pl.BlockSpec(memory_space=pl.ANY)


def load_half(index, weight_hbm, weight_ref, sems):
    half = weight_ref.shape[1]
    columns = pl.ds(pl.multiple_of(index * half, 128), half)
    parts = [slice(h, h + HEAD) for h in range(0, weight_ref.shape[0], HEAD)]
    copies = [
        pltpu.make_async_copy(weight_hbm.at[at, columns], weight_ref.at[at], sems.at[i])
        for i, at in enumerate(parts)
    ]
    for copy in copies:
        copy.start()
    for at, copy in zip(parts, copies):
        copy.wait()
        yield at


def own_half(tp, x_ref, weight_hbm, part_ref, weight_ref, sems):
    rows, block, half = x_ref.shape
    for at in load_half(tp, weight_hbm, weight_ref, sems):
        x = x_ref[...].reshape(rows * block, half)
        part_ref[:, at] = dot(x, weight_ref[at], 1, 1)


def on_core():
    return lax.rem(lax.axis_index("dp"), 2)


def begin_kernel(
    seg_hbm,
    k_hbm,
    v_hbm,
    x_hbm,
    weight_hbm,
    out_ref,
    x_ref,
    part_ref,
    turned_hbm,
    seg_ref,
    k_ref,
    v_ref,
    weight_ref,
    turned_ref,
    sems,
    weight_sems,
    turned_sems,
):
    rows, block, kv_width = k_ref.shape
    kv_heads = kv_width // HEAD
    pieces = block // TILE
    copies = [
        pltpu.make_async_copy(source, target, sems.at[i])
        for i, (source, target) in enumerate(
            ((seg_hbm, seg_ref), (k_hbm, k_ref), (v_hbm, v_ref), (x_hbm, x_ref))
        )
    ]
    for copy in copies:
        copy.start()
    copies[3].wait()

    @pl.when(on_core() == 0)
    def _():
        tp = lax.axis_index("tp")
        stores = []
        for at in load_half(1 - tp, weight_hbm, weight_ref, weight_sems):
            turned_ref[:, at] = weight_ref[at].T
            stores.append(
                pltpu.make_async_copy(
                    turned_ref.at[:, at],
                    turned_hbm.at[:, at],
                    turned_sems.at[len(stores)],
                )
            )
            stores[-1].start()
        own_half(tp, x_ref, weight_hbm, part_ref, weight_ref, weight_sems)
        for store in stores:
            store.wait()

    copies[0].wait()
    place = lax.broadcasted_iota(jnp.int32, (TILE, block), 1)
    row = lax.broadcasted_iota(jnp.int32, (TILE, block), 0)
    lane = lax.broadcasted_iota(jnp.int32, (TILE, 128), 1)
    for r in range(rows):
        spread = jnp.broadcast_to(seg_ref[r : r + 1], (TILE, block)).astype(F32)
        columns = jnp.zeros((TILE, 128), F32)
        for j in range(pieces):
            column = jnp.sum(
                jnp.where(place == row + j * TILE, spread, 0.0), axis=1, keepdims=True
            )
            columns = jnp.where(lane == j, column, columns)
        for h in range(kv_heads):
            out_ref[r * kv_heads + h, :, pieces * 2 * HEAD :] = columns.astype(BF16)
    copies[1].wait()
    copies[2].wait()
    for r in range(rows):
        for h in range(kv_heads):
            u = r * kv_heads + h
            heads = slice(h * HEAD, (h + 1) * HEAD)
            for j in range(pieces):
                at = slice(j * TILE, (j + 1) * TILE)
                k_at = j * 2 * HEAD
                out_ref[u, :, k_at : k_at + HEAD] = k_ref[r, at, heads]
                out_ref[u, :, k_at + HEAD : k_at + 2 * HEAD] = v_ref[r, at, heads]


def in_hbm(*arrays):
    return [pltpu.with_memory_space_constraint(x, pltpu.HBM) for x in arrays]


def begin(seg, k, v, x, weight):
    rows, block, kv_width = k.shape
    kv_heads = kv_width // HEAD
    lanes = block // TILE * 2 * HEAD + 128
    width, half = weight.shape[0], x.shape[2]
    return pl.pallas_call(
        begin_kernel,
        in_specs=[ANY] * 5,
        out_specs=[VMEM] * 3 + [ANY],
        out_shape=[
            pltpu.HBM((rows * kv_heads, TILE, lanes), BF16),
            jax.ShapeDtypeStruct(x.shape, BF16),
            jax.ShapeDtypeStruct((rows * block, width), F32),
            pltpu.HBM((half, width), BF16),
        ],
        scratch_shapes=[
            pltpu.VMEM(seg.shape, jnp.int32),
            pltpu.VMEM(k.shape, BF16),
            pltpu.VMEM(v.shape, BF16),
            pltpu.VMEM((width, half), BF16),
            pltpu.VMEM((half, width), BF16),
            pltpu.SemaphoreType.DMA((4,)),
            pltpu.SemaphoreType.DMA((width // HEAD,)),
            pltpu.SemaphoreType.DMA((width // HEAD,)),
        ],
        compiler_params=pltpu.CompilerParams(vmem_limit_bytes=MEDIUM_VMEM),
        name="begin",
    )(*in_hbm(seg, k, v, x, weight))


def project_own_kernel(
    x_ref, weight_hbm, turned_hbm, part_ref, turned_ref, weight_ref, sems
):
    tp = lax.axis_index("tp")

    @pl.when(on_core() == 0)
    def _():
        run_copies([pltpu.make_async_copy(turned_hbm, turned_ref, sems.at[0])])

    @pl.when(on_core() != 0)
    def _():
        for at in load_half(1 - tp, weight_hbm, weight_ref, sems):
            turned_ref[:, at] = weight_ref[at].T
        own_half(tp, x_ref, weight_hbm, part_ref, weight_ref, sems)


def project_own(x, weight, turned):
    rows, block, half = x.shape
    width = weight.shape[0]
    return pl.pallas_call(
        project_own_kernel,
        in_specs=[VMEM, ANY, ANY],
        out_specs=[VMEM, VMEM],
        out_shape=[
            jax.ShapeDtypeStruct((rows * block, width), F32),
            jax.ShapeDtypeStruct((half, width), BF16),
        ],
        scratch_shapes=[
            pltpu.VMEM((width, half), BF16),
            pltpu.SemaphoreType.DMA((width // HEAD,)),
        ],
        compiler_params=pltpu.CompilerParams(vmem_limit_bytes=MEDIUM_VMEM),
        cost_estimate=pl.CostEstimate(
            flops=2 * rows * block * half * width,
            bytes_accessed=4 * half * width,
            transcendentals=0,
        ),
        name="project_own",
    )(x, *in_hbm(weight, turned))


def other_half_kernel(x_ref, q_ref, part_0, part_1, turned_ref, out_ref):
    rows, block, half = x_ref.shape
    kv_heads = out_ref.shape[1]
    width = turned_ref.shape[1] // kv_heads
    x = x_ref[...].reshape(rows * block, half)
    for h in range(kv_heads):
        at = slice(h * width, (h + 1) * width)
        out_ref[:, h, :, :width] = q_ref[:, :, at]
        part = jnp.where(on_core() == 0, part_0[:, at], part_1[:, at])
        total = part + dot(x, turned_ref[:, at], 1, 0)
        out_ref[:, h, :, width:] = total.astype(BF16).reshape(rows, block, width)


def project_other(x, q, part_0, part_1, turned, kv_heads):
    rows, block, half = x.shape
    total = turned.shape[1]
    return pl.pallas_call(
        other_half_kernel,
        in_specs=[VMEM] * 5,
        out_specs=VMEM,
        out_shape=pltpu.HBM((rows, kv_heads, block, 2 * total // kv_heads), BF16),
        compiler_params=pltpu.CompilerParams(vmem_limit_bytes=MEDIUM_VMEM),
        cost_estimate=pl.CostEstimate(
            flops=2 * rows * block * half * total,
            bytes_accessed=2 * half * total,
            transcendentals=0,
        ),
        name="project_other",
    )(x, q, part_0, part_1, turned)


def attention_kernel(
    own_ref,
    other_ref,
    qd_ref,
    dq_hbm,
    dkv_own,
    dkv_other,
    acc,
    dq_ref,
    sems,
):
    steps, block, width = dq_ref.shape
    per = 2
    lanes = per * block
    pieces = block // TILE
    side = lax.rem(lax.axis_index("ctx"), 2)

    def gathered(ref, low, high, start):
        return jnp.concatenate(
            [
                ref[SLOT[z], :, start + j * 2 * HEAD : start + j * 2 * HEAD + HEAD]
                for z in range(low, high)
                for j in range(pieces)
            ],
            axis=0,
        )

    def ids(ref, low, high):
        return jnp.concatenate(
            [
                ref[SLOT[z], :, pieces * 2 * HEAD :].astype(F32)[:, j : j + 1]
                for z in range(low, high)
                for j in range(pieces)
            ],
            axis=0,
        )

    def positions(shape, axis, low, which):
        n = lax.broadcasted_iota(jnp.int32, shape, axis)
        return 2 * n - (n & (block - 1)) + (per * block * low + block * which)

    diagonal = lax.broadcasted_iota(
        jnp.int32, (lanes, lanes), 0
    ) == lax.broadcasted_iota(jnp.int32, (lanes, lanes), 1)

    def scores(z):
        low, high = max(0, z - 4), z + per
        qd = jnp.concatenate([qd_ref[SLOT[i]] for i in range(z, high)], axis=0)
        q = jnp.concatenate([qd[:, :HEAD], qd[:, HEAD:width]], axis=0)
        do = jnp.concatenate(
            [qd[:, width : width + HEAD], qd[:, width + HEAD :]], axis=0
        )
        seg_q = ids(own_ref, z, high)
        seg_q = jnp.sum(jnp.where(diagonal, seg_q, 0.0), axis=0, keepdims=True)
        pos_q = positions((1, lanes), 1, z, side)
        parts = []
        total = 0.0
        weighted = 0.0
        for which, ref in enumerate((own_ref, other_ref)):
            for start, stop in ((low, z), (z, high)):
                if start == stop:
                    continue
                k = gathered(ref, start, stop, 0)
                v = gathered(ref, start, stop, HEAD)
                allowed = ids(ref, start, stop) == seg_q
                if start == z:
                    key_side = side if which == 0 else 1 - side
                    pos_k = positions((lanes, lanes), 0, z, key_side)
                    allowed &= pos_k <= pos_q
                allowed = jnp.concatenate([allowed, allowed], axis=1)
                t = jnp.tanh(dot(k, q, 1, 1) * (SCALE / CAP))
                e = jnp.where(allowed, jnp.exp2(t * (CAP * LOG2E)), 0.0)
                dp = dot(v, do, 1, 1)
                total += jnp.sum(e, axis=0, keepdims=True)
                weighted += jnp.sum(e * dp, axis=0, keepdims=True)
                parts.append((which, start, stop, k, t, e, dp))
        return z, q, do, parts, total, weighted

    def gradients(z, q, do, parts, total, weighted):
        inverse = 1.0 / total
        delta = weighted * inverse
        dq = 0.0
        for which, start, stop, k, t, e, dp in parts:
            prob = e * inverse
            ds = (prob * (dp - delta) * (1.0 - t * t)).astype(BF16)
            at = slice(start * block, stop * block)
            dk, dv = dot(ds, q, 1, 0), dot(prob.astype(BF16), do, 1, 0)
            if z == start:
                acc[which, at, :HEAD] = dk
                acc[which, at, HEAD:] = dv
            else:
                acc[which, at, :HEAD] += dk
                acc[which, at, HEAD:] += dv
            dq += dot(ds, k, 0, 0)
        dq = (dq * SCALE).astype(BF16)
        for i in range(per):
            at = slice(i * block, (i + 1) * block)
            slot = SLOT[z + i]
            dq_ref[slot, :, :HEAD] = dq[:lanes][at]
            dq_ref[slot, :, HEAD:] = dq[lanes:][at]
            copies.append(
                pltpu.make_async_copy(dq_ref.at[slot], dq_hbm.at[slot], sems.at[slot])
            )
            copies[-1].start()

    held = None
    copies = []
    for z in range(0, steps, per):
        ready = scores(z)
        if held is not None:
            gradients(*held)
        held = ready
    gradients(*held)
    for z in range(steps):
        at = slice(z * block, (z + 1) * block)
        for which, out_ref in enumerate((dkv_own, dkv_other)):
            out_ref[SLOT[z], :, :HEAD] = (acc[which, at, :HEAD] * SCALE).astype(BF16)
            out_ref[SLOT[z], :, HEAD:] = acc[which, at, HEAD:].astype(BF16)
    for copy in copies:
        copy.wait()


def attention(own, other, q_and_grad):
    steps, block, width = q_and_grad.shape
    width //= 2
    return pl.pallas_call(
        attention_kernel,
        in_specs=[VMEM] * 3,
        out_specs=[ANY, VMEM, VMEM],
        out_shape=[
            pltpu.HBM((steps, block, width), BF16),
            pltpu.VMEM((steps, block, width), BF16),
            pltpu.VMEM((steps, block, width), BF16),
        ],
        scratch_shapes=[
            pltpu.VMEM((2, steps * block, width), F32),
            pltpu.VMEM((steps, block, width), BF16),
            pltpu.SemaphoreType.DMA((steps,)),
        ],
        compiler_params=pltpu.CompilerParams(vmem_limit_bytes=LARGE_VMEM),
        cost_estimate=pl.CostEstimate(
            flops=3 * 10**9, bytes_accessed=6 * 2**20, transcendentals=1200000
        ),
        name="attend",
    )(own, other, q_and_grad)


def run_copies(copies):
    for copy in copies:
        copy.start()
    for copy in copies:
        copy.wait()


def pick_kernel(index_ref, in_ref, *outs):
    for i, out in enumerate(outs):

        @pl.when(index_ref[i] >= 0)
        def _():
            out[...] = in_ref[index_ref[i]]


def pick_rows(index, source):
    count, rest = index.shape[0], source.shape[1:]
    return pl.pallas_call(
        pick_kernel,
        in_specs=[SMEM, VMEM],
        out_specs=[VMEM] * count,
        out_shape=[jax.ShapeDtypeStruct(rest, source.dtype)] * count,
        compiler_params=pltpu.CompilerParams(vmem_limit_bytes=SMALL_VMEM),
        name="pick",
    )(index, source)


def pick_stacked_kernel(index_ref, in_ref, out_ref, sems):
    def each(act):
        for i in range(out_ref.shape[0]):

            @pl.when(index_ref[i] >= 0)
            def _():
                act(
                    pltpu.make_async_copy(
                        in_ref.at[index_ref[i]], out_ref.at[i], sems.at[i]
                    )
                )

    each(lambda copy: copy.start())
    each(lambda copy: copy.wait())


def pick_stacked(index, source):
    count, rest = index.shape[0], source.shape[1:]
    return pl.pallas_call(
        pick_stacked_kernel,
        in_specs=[SMEM, VMEM],
        out_specs=ANY,
        out_shape=jax.ShapeDtypeStruct((count,) + rest, source.dtype),
        scratch_shapes=[pltpu.SemaphoreType.DMA((count,))],
        compiler_params=pltpu.CompilerParams(vmem_limit_bytes=SMALL_VMEM),
        name="pick_stacked",
    )(index, source)


def place_q_kernel(index_ref, *refs):
    ins, out_ref, sems = refs[:-2], refs[-2], refs[-1]
    kv_heads, _, width = ins[0].shape

    def copy(source, s, h):
        return pltpu.make_async_copy(
            source.at[h], out_ref.at[s, :, pl.ds(h * width, width)], sems.at[s, h]
        )

    for s in range(out_ref.shape[0]):
        for i, source in enumerate(ins):

            @pl.when(index_ref[s] == i)
            def _():
                for h in range(kv_heads):
                    copy(source, s, h).start()

    for s in range(out_ref.shape[0]):
        for h in range(kv_heads):
            copy(ins[0], s, h).wait()


def place_q(index, sources):
    count = index.shape[0]
    kv_heads, block, width = sources[0].shape
    return pl.pallas_call(
        place_q_kernel,
        in_specs=[SMEM] + [VMEM] * len(sources),
        out_specs=ANY,
        out_shape=jax.ShapeDtypeStruct((count, block, kv_heads * width), BF16),
        scratch_shapes=[pltpu.SemaphoreType.DMA((count, kv_heads))],
        compiler_params=pltpu.CompilerParams(vmem_limit_bytes=SMALL_VMEM),
        name="place_q",
    )(index, *sources)


def place_kv_kernel(index_ref, in_ref, key_ref, value_ref, sems):
    copies = []
    for s in range(key_ref.shape[0]):
        for h in range(in_ref.shape[1]):
            for w, out_ref in enumerate((key_ref, value_ref)):
                copies.append(
                    pltpu.make_async_copy(
                        in_ref.at[index_ref[s], h, :, pl.ds(w * HEAD, HEAD)],
                        out_ref.at[s, :, pl.ds(h * HEAD, HEAD)],
                        sems.at[s, h, w],
                    )
                )
    run_copies(copies)


def place_kv(index, source):
    count = index.shape[0]
    _, kv_heads, block, _ = source.shape
    return pl.pallas_call(
        place_kv_kernel,
        in_specs=[SMEM, VMEM],
        out_specs=[ANY] * 2,
        out_shape=[jax.ShapeDtypeStruct((count, block, kv_heads * HEAD), BF16)] * 2,
        scratch_shapes=[pltpu.SemaphoreType.DMA((count, kv_heads, 2))],
        compiler_params=pltpu.CompilerParams(vmem_limit_bytes=SMALL_VMEM),
        name="place_kv",
    )(index, source)


def exchange(x, axis, groups=None):
    return lax.all_to_all(
        x, axis, split_axis=0, concat_axis=0, tiled=True, axis_index_groups=groups
    )


def on_device(
    queries, key_states, value_state_rows, segment_ids, output_grad, out_weight, destination
):
    rows, block, q_width = queries.shape
    kv_heads = key_states.shape[2] // HEAD
    units = rows * kv_heads
    n_ctx = lax.axis_size("ctx")
    groups = lax.axis_size("dp")
    pair = n_ctx // units
    ctx = lax.axis_index("ctx")
    group = lax.axis_index("dp")
    side = ctx % pair
    columns = [[z * pair + h for z in ORDER] for h in range(pair)]
    swap = [(z * pair + h, z * pair + 1 - h) for z in range(units) for h in range(pair)]

    own, grad, part_0, turned = begin(
        segment_ids, key_states, value_state_rows, output_grad, out_weight
    )
    other_grad = lax.ppermute(grad, "tp", [(0, 1), (1, 0)])
    own = exchange(own, "ctx", columns)
    other = lax.ppermute(own, "ctx", swap)

    def partner(g, i, sign):
        chips = groups // 2
        return (g // 2 + sign * (i // 2) + chips) % chips * 2 + (g % 2 + i) % 2

    steps = jnp.arange(groups, dtype=jnp.int32)
    dest = destination.reshape(groups, rows)
    own_targets = lax.dynamic_slice_in_dim(dest, group, 1, 0) // rows

    def row_for(targets):
        return (
            jnp.sum(
                jnp.where(
                    own_targets == targets[:, None],
                    jnp.arange(1, rows + 1, dtype=jnp.int32)[None, :],
                    0,
                ),
                axis=1,
            )
            - 1
        )

    wanted = group * rows + jnp.arange(rows, dtype=jnp.int32)
    recv_index = jnp.sum(
        jnp.where(
            destination[None, :] == wanted[:, None],
            jnp.arange(groups * rows, dtype=jnp.int32)[None, :] // rows,
            0,
        ),
        axis=1,
    )
    recv_step = jnp.sum(
        jnp.where(recv_index[:, None] == partner(group, steps, -1)[None, :], steps, 0),
        axis=1,
    )
    send_index = row_for(steps)
    send_step = row_for(partner(group, steps, 1))

    part_1, turned = project_own(grad, out_weight, turned)
    q_and_grad = project_other(
        other_grad, queries, part_0, part_1, turned, kv_heads
    )
    q_and_grad = q_and_grad.reshape(units, block, q_and_grad.shape[3])
    q_and_grad = exchange(q_and_grad, "ctx", columns)

    dq, dkv_mine, dkv_theirs = attention(own, other, q_and_grad)

    dkv_back = lax.ppermute(dkv_theirs, "ctx", swap)
    dq = exchange(dq, "ctx", columns)
    dkv = (dkv_mine.astype(F32) + dkv_back.astype(F32)).astype(BF16)
    dkv, dq = lax.optimization_barrier((dkv, dq))
    dkv = exchange(dkv, "ctx", columns)

    def by_row(x):
        return x.reshape(rows, kv_heads, block, x.shape[2])

    sent = pick_rows(send_step, by_row(dq))
    got = [sent[0]]
    for i in range(1, groups):
        route = [(g, partner(g, i, 1)) for g in range(groups)]
        got.append(lax.ppermute(sent[i], "dp", route))
    dkv, *got = lax.optimization_barrier((dkv, *got))
    query_out = place_q(recv_step, got)
    dkv = exchange(pick_stacked(send_index, by_row(dkv)), "dp")
    key_out, value_out = place_kv(recv_index, dkv)
    return query_out, key_out, value_out


def solution(mesh):
    in_specs = (
        P("dp", "ctx", "tp"),
        P("dp", "ctx", "tp"),
        P("dp", "ctx", "tp"),
        P("dp", "ctx"),
        P("dp", "ctx", "tp"),
        P("tp", None),
        P(),
    )
    out_specs = (P("dp", "ctx", "tp"), P("dp", "ctx", "tp"), P("dp", "ctx", "tp"))
    return jax.shard_map(
        on_device, mesh=mesh, in_specs=in_specs, out_specs=out_specs, check_vma=False
    )
```

```python
import jax
import jax.numpy as jnp
from jax import lax
from jax.experimental import pallas as pl
from jax.experimental.pallas import tpu as pltpu
from jax.sharding import PartitionSpec as P

HEAD = 256
CAP = 50.0
SCALE = 0.0625
LOG2E = 1.4426950408889634
F32 = jnp.float32
BF16 = jnp.bfloat16
TILE = 16
ORDER = (0, 4, 1, 5, 2, 6, 3, 7)
SLOT = tuple(ORDER.index(z) for z in range(len(ORDER)))
SMALL_VMEM = 8 * 1024 * 1024
MEDIUM_VMEM = 14 * 1024 * 1024
LARGE_VMEM = 28 * 1024 * 1024


def dot(a, b, ca, cb):
    return lax.dot_general(a, b, (((ca,), (cb,)), ((), ())), preferred_element_type=F32)


VMEM = pl.BlockSpec(memory_space=pltpu.VMEM)
SMEM = pl.BlockSpec(memory_space=pltpu.SMEM)
ANY = pl.BlockSpec(memory_space=pl.ANY)


def load_half(index, weight_hbm, weight_ref, sems):
    half = weight_ref.shape[1]
    columns = pl.ds(pl.multiple_of(index * half, 128), half)
    parts = [slice(h, h + HEAD) for h in range(0, weight_ref.shape[0], HEAD)]
    copies = [
        pltpu.make_async_copy(weight_hbm.at[at, columns], weight_ref.at[at], sems.at[i])
        for i, at in enumerate(parts)
    ]
    for copy in copies:
        copy.start()
    for at, copy in zip(parts, copies):
        copy.wait()
        yield at


def own_half(tp, x_ref, weight_hbm, part_ref, weight_ref, sems):
    rows, block, half = x_ref.shape
    for at in load_half(tp, weight_hbm, weight_ref, sems):
        x = x_ref[...].reshape(rows * block, half)
        part_ref[:, at] = dot(x, weight_ref[at], 1, 1)


def on_core():
    return lax.rem(lax.axis_index("dp"), 2)


def begin_kernel(
    seg_hbm,
    k_hbm,
    v_hbm,
    x_hbm,
    weight_hbm,
    out_ref,
    x_ref,
    part_ref,
    turned_hbm,
    seg_ref,
    k_ref,
    v_ref,
    weight_ref,
    turned_ref,
    sems,
    weight_sems,
    turned_sems,
):
    rows, block, kv_width = k_ref.shape
    kv_heads = kv_width // HEAD
    pieces = block // TILE
    copies = [
        pltpu.make_async_copy(source, target, sems.at[i])
        for i, (source, target) in enumerate(
            ((seg_hbm, seg_ref), (k_hbm, k_ref), (v_hbm, v_ref), (x_hbm, x_ref))
        )
    ]
    for copy in copies:
        copy.start()
    copies[3].wait()

    @pl.when(on_core() == 0)
    def _():
        tp = lax.axis_index("tp")
        own_half(tp, x_ref, weight_hbm, part_ref, weight_ref, weight_sems)
        stores = []
        for at in load_half(1 - tp, weight_hbm, weight_ref, weight_sems):
            turned_ref[:, at] = weight_ref[at].T
            stores.append(
                pltpu.make_async_copy(
                    turned_ref.at[:, at],
                    turned_hbm.at[:, at],
                    turned_sems.at[len(stores)],
                )
            )
            stores[-1].start()
        for store in stores:
            store.wait()

    copies[0].wait()
    place = lax.broadcasted_iota(jnp.int32, (TILE, block), 1)
    row = lax.broadcasted_iota(jnp.int32, (TILE, block), 0)
    lane = lax.broadcasted_iota(jnp.int32, (TILE, 128), 1)
    for r in range(rows):
        spread = jnp.broadcast_to(seg_ref[r : r + 1], (TILE, block)).astype(F32)
        columns = jnp.zeros((TILE, 128), F32)
        for j in range(pieces):
            column = jnp.sum(
                jnp.where(place == row + j * TILE, spread, 0.0), axis=1, keepdims=True
            )
            columns = jnp.where(lane == j, column, columns)
        for h in range(kv_heads):
            out_ref[r * kv_heads + h, :, pieces * 2 * HEAD :] = columns.astype(BF16)
    copies[1].wait()
    copies[2].wait()
    for r in range(rows):
        for h in range(kv_heads):
            u = r * kv_heads + h
            heads = slice(h * HEAD, (h + 1) * HEAD)
            for j in range(pieces):
                at = slice(j * TILE, (j + 1) * TILE)
                k_at = j * 2 * HEAD
                out_ref[u, :, k_at : k_at + HEAD] = k_ref[r, at, heads]
                out_ref[u, :, k_at + HEAD : k_at + 2 * HEAD] = v_ref[r, at, heads]


def in_hbm(*arrays):
    return [pltpu.with_memory_space_constraint(x, pltpu.HBM) for x in arrays]


def begin(seg, k, v, x, weight):
    rows, block, kv_width = k.shape
    kv_heads = kv_width // HEAD
    lanes = block // TILE * 2 * HEAD + 128
    width, half = weight.shape[0], x.shape[2]
    return pl.pallas_call(
        begin_kernel,
        in_specs=[ANY] * 5,
        out_specs=[VMEM] * 3 + [ANY],
        out_shape=[
            pltpu.HBM((rows * kv_heads, TILE, lanes), BF16),
            jax.ShapeDtypeStruct(x.shape, BF16),
            jax.ShapeDtypeStruct((rows * block, width), F32),
            pltpu.HBM((half, width), BF16),
        ],
        scratch_shapes=[
            pltpu.VMEM(seg.shape, jnp.int32),
            pltpu.VMEM(k.shape, BF16),
            pltpu.VMEM(v.shape, BF16),
            pltpu.VMEM((width, half), BF16),
            pltpu.VMEM((half, width), BF16),
            pltpu.SemaphoreType.DMA((4,)),
            pltpu.SemaphoreType.DMA((width // HEAD,)),
            pltpu.SemaphoreType.DMA((width // HEAD,)),
        ],
        compiler_params=pltpu.CompilerParams(vmem_limit_bytes=MEDIUM_VMEM),
        name="begin",
    )(*in_hbm(seg, k, v, x, weight))


def project_own_kernel(
    x_ref, weight_hbm, turned_hbm, part_ref, turned_ref, weight_ref, sems
):
    tp = lax.axis_index("tp")

    @pl.when(on_core() == 0)
    def _():
        run_copies([pltpu.make_async_copy(turned_hbm, turned_ref, sems.at[0])])

    @pl.when(on_core() != 0)
    def _():
        for at in load_half(1 - tp, weight_hbm, weight_ref, sems):
            turned_ref[:, at] = weight_ref[at].T
        own_half(tp, x_ref, weight_hbm, part_ref, weight_ref, sems)


def project_own(x, weight, turned):
    rows, block, half = x.shape
    width = weight.shape[0]
    return pl.pallas_call(
        project_own_kernel,
        in_specs=[VMEM, ANY, ANY],
        out_specs=[VMEM, VMEM],
        out_shape=[
            jax.ShapeDtypeStruct((rows * block, width), F32),
            jax.ShapeDtypeStruct((half, width), BF16),
        ],
        scratch_shapes=[
            pltpu.VMEM((width, half), BF16),
            pltpu.SemaphoreType.DMA((width // HEAD,)),
        ],
        compiler_params=pltpu.CompilerParams(vmem_limit_bytes=MEDIUM_VMEM),
        cost_estimate=pl.CostEstimate(
            flops=2 * rows * block * half * width,
            bytes_accessed=4 * half * width,
            transcendentals=0,
        ),
        name="project_own",
    )(x, *in_hbm(weight, turned))


def other_half_kernel(x_ref, q_ref, part_0, part_1, turned_ref, out_ref):
    rows, block, half = x_ref.shape
    kv_heads = out_ref.shape[1]
    width = turned_ref.shape[1] // kv_heads
    x = x_ref[...].reshape(rows * block, half)
    for h in range(kv_heads):
        at = slice(h * width, (h + 1) * width)
        out_ref[:, h, :, :width] = q_ref[:, :, at]
        part = jnp.where(on_core() == 0, part_0[:, at], part_1[:, at])
        total = part + dot(x, turned_ref[:, at], 1, 0)
        out_ref[:, h, :, width:] = total.astype(BF16).reshape(rows, block, width)


def project_other(x, q, part_0, part_1, turned, kv_heads):
    rows, block, half = x.shape
    total = turned.shape[1]
    return pl.pallas_call(
        other_half_kernel,
        in_specs=[VMEM] * 5,
        out_specs=VMEM,
        out_shape=pltpu.HBM((rows, kv_heads, block, 2 * total // kv_heads), BF16),
        compiler_params=pltpu.CompilerParams(vmem_limit_bytes=MEDIUM_VMEM),
        cost_estimate=pl.CostEstimate(
            flops=2 * rows * block * half * total,
            bytes_accessed=2 * half * total,
            transcendentals=0,
        ),
        name="project_other",
    )(x, q, part_0, part_1, turned)


def attention_kernel(
    own_ref,
    other_ref,
    qd_ref,
    dq_hbm,
    dkv_own,
    dkv_other,
    acc,
    dq_ref,
    sems,
):
    steps, block, width = dq_ref.shape
    per = 2
    lanes = per * block
    pieces = block // TILE
    side = lax.rem(lax.axis_index("ctx"), 2)

    def gathered(ref, low, high, start):
        return jnp.concatenate(
            [
                ref[SLOT[z], :, start + j * 2 * HEAD : start + j * 2 * HEAD + HEAD]
                for z in range(low, high)
                for j in range(pieces)
            ],
            axis=0,
        )

    def ids(ref, low, high):
        return jnp.concatenate(
            [
                ref[SLOT[z], :, pieces * 2 * HEAD :].astype(F32)[:, j : j + 1]
                for z in range(low, high)
                for j in range(pieces)
            ],
            axis=0,
        )

    def positions(shape, axis, low, which):
        n = lax.broadcasted_iota(jnp.int32, shape, axis)
        return 2 * n - (n & (block - 1)) + (per * block * low + block * which)

    diagonal = lax.broadcasted_iota(
        jnp.int32, (lanes, lanes), 0
    ) == lax.broadcasted_iota(jnp.int32, (lanes, lanes), 1)

    def scores(z):
        low, high = max(0, z - 4), z + per
        qd = jnp.concatenate([qd_ref[SLOT[i]] for i in range(z, high)], axis=0)
        q = jnp.concatenate([qd[:, :HEAD], qd[:, HEAD:width]], axis=0)
        do = jnp.concatenate(
            [qd[:, width : width + HEAD], qd[:, width + HEAD :]], axis=0
        )
        seg_q = ids(own_ref, z, high)
        seg_q = jnp.sum(jnp.where(diagonal, seg_q, 0.0), axis=0, keepdims=True)
        pos_q = positions((1, lanes), 1, z, side)
        parts = []
        total = 0.0
        weighted = 0.0
        for which, ref in enumerate((own_ref, other_ref)):
            for start, stop in ((low, z), (z, high)):
                if start == stop:
                    continue
                k = gathered(ref, start, stop, 0)
                v = gathered(ref, start, stop, HEAD)
                allowed = ids(ref, start, stop) == seg_q
                if start == z:
                    key_side = side if which == 0 else 1 - side
                    pos_k = positions((lanes, lanes), 0, z, key_side)
                    allowed &= pos_k <= pos_q
                allowed = jnp.concatenate([allowed, allowed], axis=1)
                t = jnp.tanh(dot(k, q, 1, 1) * (SCALE / CAP))
                e = jnp.where(allowed, jnp.exp2(t * (CAP * LOG2E)), 0.0)
                dp = dot(v, do, 1, 1)
                total += jnp.sum(e, axis=0, keepdims=True)
                weighted += jnp.sum(e * dp, axis=0, keepdims=True)
                parts.append((which, start, stop, k, t, e, dp))
        return z, q, do, parts, total, weighted

    def gradients(z, q, do, parts, total, weighted):
        inverse = 1.0 / total
        delta = weighted * inverse
        dq = 0.0
        for which, start, stop, k, t, e, dp in parts:
            prob = e * inverse
            ds = (prob * (dp - delta) * (1.0 - t * t)).astype(BF16)
            at = slice(start * block, stop * block)
            dk, dv = dot(ds, q, 1, 0), dot(prob.astype(BF16), do, 1, 0)
            if z == start:
                acc[which, at, :HEAD] = dk
                acc[which, at, HEAD:] = dv
            else:
                acc[which, at, :HEAD] += dk
                acc[which, at, HEAD:] += dv
            dq += dot(ds, k, 0, 0)
        dq = (dq * SCALE).astype(BF16)
        for i in range(per):
            at = slice(i * block, (i + 1) * block)
            slot = SLOT[z + i]
            dq_ref[slot, :, :HEAD] = dq[:lanes][at]
            dq_ref[slot, :, HEAD:] = dq[lanes:][at]
            copies.append(
                pltpu.make_async_copy(dq_ref.at[slot], dq_hbm.at[slot], sems.at[slot])
            )
            copies[-1].start()

    held = None
    copies = []
    for z in range(0, steps, per):
        ready = scores(z)
        if held is not None:
            gradients(*held)
        held = ready
    gradients(*held)
    for z in range(steps):
        at = slice(z * block, (z + 1) * block)
        for which, out_ref in enumerate((dkv_own, dkv_other)):
            out_ref[SLOT[z], :, :HEAD] = (acc[which, at, :HEAD] * SCALE).astype(BF16)
            out_ref[SLOT[z], :, HEAD:] = acc[which, at, HEAD:].astype(BF16)
    for copy in copies:
        copy.wait()


def attention(own, other, q_and_grad):
    steps, block, width = q_and_grad.shape
    width //= 2
    return pl.pallas_call(
        attention_kernel,
        in_specs=[VMEM] * 3,
        out_specs=[ANY, VMEM, VMEM],
        out_shape=[
            pltpu.HBM((steps, block, width), BF16),
            pltpu.VMEM((steps, block, width), BF16),
            pltpu.VMEM((steps, block, width), BF16),
        ],
        scratch_shapes=[
            pltpu.VMEM((2, steps * block, width), F32),
            pltpu.VMEM((steps, block, width), BF16),
            pltpu.SemaphoreType.DMA((steps,)),
        ],
        compiler_params=pltpu.CompilerParams(vmem_limit_bytes=LARGE_VMEM),
        cost_estimate=pl.CostEstimate(
            flops=3 * 10**9, bytes_accessed=6 * 2**20, transcendentals=1200000
        ),
        name="attend",
    )(own, other, q_and_grad)


def run_copies(copies):
    for copy in copies:
        copy.start()
    for copy in copies:
        copy.wait()


def pick_kernel(index_ref, in_ref, *outs):
    for i, out in enumerate(outs):

        @pl.when(index_ref[i] >= 0)
        def _():
            out[...] = in_ref[index_ref[i]]


def pick_rows(index, source):
    count, rest = index.shape[0], source.shape[1:]
    return pl.pallas_call(
        pick_kernel,
        in_specs=[SMEM, VMEM],
        out_specs=[VMEM] * count,
        out_shape=[jax.ShapeDtypeStruct(rest, source.dtype)] * count,
        compiler_params=pltpu.CompilerParams(vmem_limit_bytes=SMALL_VMEM),
        name="pick",
    )(index, source)


def pick_stacked_kernel(index_ref, in_ref, out_ref, sems):
    def each(act):
        for i in range(out_ref.shape[0]):

            @pl.when(index_ref[i] >= 0)
            def _():
                act(
                    pltpu.make_async_copy(
                        in_ref.at[index_ref[i]], out_ref.at[i], sems.at[i]
                    )
                )

    each(lambda copy: copy.start())
    each(lambda copy: copy.wait())


def pick_stacked(index, source):
    count, rest = index.shape[0], source.shape[1:]
    return pl.pallas_call(
        pick_stacked_kernel,
        in_specs=[SMEM, VMEM],
        out_specs=ANY,
        out_shape=jax.ShapeDtypeStruct((count,) + rest, source.dtype),
        scratch_shapes=[pltpu.SemaphoreType.DMA((count,))],
        compiler_params=pltpu.CompilerParams(vmem_limit_bytes=SMALL_VMEM),
        name="pick_stacked",
    )(index, source)


def place_q_kernel(index_ref, *refs):
    ins, out_ref, sems = refs[:-2], refs[-2], refs[-1]
    kv_heads, _, width = ins[0].shape

    def copy(source, s, h):
        return pltpu.make_async_copy(
            source.at[h], out_ref.at[s, :, pl.ds(h * width, width)], sems.at[s, h]
        )

    for s in range(out_ref.shape[0]):
        for i, source in enumerate(ins):

            @pl.when(index_ref[s] == i)
            def _():
                for h in range(kv_heads):
                    copy(source, s, h).start()

    for s in range(out_ref.shape[0]):
        for h in range(kv_heads):
            copy(ins[0], s, h).wait()


def place_q(index, sources):
    count = index.shape[0]
    kv_heads, block, width = sources[0].shape
    return pl.pallas_call(
        place_q_kernel,
        in_specs=[SMEM] + [VMEM] * len(sources),
        out_specs=ANY,
        out_shape=jax.ShapeDtypeStruct((count, block, kv_heads * width), BF16),
        scratch_shapes=[pltpu.SemaphoreType.DMA((count, kv_heads))],
        compiler_params=pltpu.CompilerParams(vmem_limit_bytes=SMALL_VMEM),
        name="place_q",
    )(index, *sources)


def place_kv_kernel(index_ref, in_ref, key_ref, value_ref, sems):
    copies = []
    for s in range(key_ref.shape[0]):
        for h in range(in_ref.shape[1]):
            for w, out_ref in enumerate((key_ref, value_ref)):
                copies.append(
                    pltpu.make_async_copy(
                        in_ref.at[index_ref[s], h, :, pl.ds(w * HEAD, HEAD)],
                        out_ref.at[s, :, pl.ds(h * HEAD, HEAD)],
                        sems.at[s, h, w],
                    )
                )
    run_copies(copies)


def place_kv(index, source):
    count = index.shape[0]
    _, kv_heads, block, _ = source.shape
    return pl.pallas_call(
        place_kv_kernel,
        in_specs=[SMEM, VMEM],
        out_specs=[ANY] * 2,
        out_shape=[jax.ShapeDtypeStruct((count, block, kv_heads * HEAD), BF16)] * 2,
        scratch_shapes=[pltpu.SemaphoreType.DMA((count, kv_heads, 2))],
        compiler_params=pltpu.CompilerParams(vmem_limit_bytes=SMALL_VMEM),
        name="place_kv",
    )(index, source)


def exchange(x, axis, groups=None):
    return lax.all_to_all(
        x, axis, split_axis=0, concat_axis=0, tiled=True, axis_index_groups=groups
    )


def on_device(
    queries, key_states, value_state_rows, segment_ids, output_grad, out_weight, destination
):
    rows, block, q_width = queries.shape
    kv_heads = key_states.shape[2] // HEAD
    units = rows * kv_heads
    n_ctx = lax.axis_size("ctx")
    groups = lax.axis_size("dp")
    pair = n_ctx // units
    ctx = lax.axis_index("ctx")
    group = lax.axis_index("dp")
    side = ctx % pair
    columns = [[z * pair + h for z in ORDER] for h in range(pair)]
    swap = [(z * pair + h, z * pair + 1 - h) for z in range(units) for h in range(pair)]

    own, grad, part_0, turned = begin(
        segment_ids, key_states, value_state_rows, output_grad, out_weight
    )
    other_grad = lax.ppermute(grad, "tp", [(0, 1), (1, 0)])
    own = exchange(own, "ctx", columns)
    other = lax.ppermute(own, "ctx", swap)

    def partner(g, i, sign):
        chips = groups // 2
        return (g // 2 + sign * (i // 2) + chips) % chips * 2 + (g % 2 + i) % 2

    steps = jnp.arange(groups, dtype=jnp.int32)
    dest = destination.reshape(groups, rows)
    own_targets = lax.dynamic_slice_in_dim(dest, group, 1, 0) // rows

    def row_for(targets):
        return (
            jnp.sum(
                jnp.where(
                    own_targets == targets[:, None],
                    jnp.arange(1, rows + 1, dtype=jnp.int32)[None, :],
                    0,
                ),
                axis=1,
            )
            - 1
        )

    wanted = group * rows + jnp.arange(rows, dtype=jnp.int32)
    recv_index = jnp.sum(
        jnp.where(
            destination[None, :] == wanted[:, None],
            jnp.arange(groups * rows, dtype=jnp.int32)[None, :] // rows,
            0,
        ),
        axis=1,
    )
    recv_step = jnp.sum(
        jnp.where(recv_index[:, None] == partner(group, steps, -1)[None, :], steps, 0),
        axis=1,
    )
    order = jnp.array(ORDER, jnp.int32)
    send_index = row_for(order)
    recv_index = jnp.sum(
        jnp.where(recv_index[:, None] == order[None, :], steps[None, :], 0), axis=1
    )
    send_step = row_for(partner(group, steps, 1))

    part_1, turned = project_own(grad, out_weight, turned)
    q_and_grad = project_other(
        other_grad, queries, part_0, part_1, turned, kv_heads
    )
    q_and_grad = q_and_grad.reshape(units, block, q_and_grad.shape[3])
    q_and_grad = exchange(q_and_grad, "ctx", columns)

    dq, dkv_mine, dkv_theirs = attention(own, other, q_and_grad)

    dkv_back = lax.ppermute(dkv_theirs, "ctx", swap)
    dq = exchange(dq, "ctx", columns)
    dkv = (dkv_mine.astype(F32) + dkv_back.astype(F32)).astype(BF16)
    dkv, dq = lax.optimization_barrier((dkv, dq))
    dkv = exchange(dkv, "ctx", columns)

    def by_row(x):
        return x.reshape(rows, kv_heads, block, x.shape[2])

    sent = pick_rows(send_step, by_row(dq))
    got = [sent[0]]
    for i in range(1, groups):
        route = [(g, partner(g, i, 1)) for g in range(groups)]
        got.append(lax.ppermute(sent[i], "dp", route))
    dkv, *got = lax.optimization_barrier((dkv, *got))
    query_out = place_q(recv_step, got)
    dkv = exchange(pick_stacked(send_index, by_row(dkv)), "dp", [list(ORDER)])
    key_out, value_out = place_kv(recv_index, dkv)
    return query_out, key_out, value_out


def solution(mesh):
    in_specs = (
        P("dp", "ctx", "tp"),
        P("dp", "ctx", "tp"),
        P("dp", "ctx", "tp"),
        P("dp", "ctx"),
        P("dp", "ctx", "tp"),
        P("tp", None),
        P(),
    )
    out_specs = (P("dp", "ctx", "tp"), P("dp", "ctx", "tp"), P("dp", "ctx", "tp"))
    return jax.shard_map(
        on_device, mesh=mesh, in_specs=in_specs, out_specs=out_specs, check_vma=False
    )
```
